128 devices in a mesh: win: 4 (over z_hi, core), chan: 32 (over x, z_lo, y).
Axes of the slice: x: 4, y: 4, z: 4 (z_hi: 2, z_lo: 2; z = z_hi * 2 + z_lo), core: 2. Of those that a mesh axis runs over, the one named last changes fastest.
Arguments:
- record: bfloat16 [12, 7936, 8192], P('win', 'chan'), may hold values from -6 to 6
- offsets: int32 [12], P('win'), may hold values from 0 to 256
- sources: int32 [3, 16], replicated, may hold values from 0 to 8191
Outputs:
- correlations: bfloat16 [3, 16, 256, 8192], P(None, 'win', None, 'chan')
The draws below stay inside these ranges and needn't reach their ends.
Inputs may be any that keep to these rules, and one draw needn't show every extreme that they name: `sources`: channels may repeat within a round.
All inputs are finite; a program needn't handle non-finite values.
Results may differ from the reference program's by a relative error of at most 0.0061.
Values may be sent and summed in bfloat16 or wider, within the bound.
A program may use at most 192 MiB of HBM per device.

```python
import math
import jax
import jax.numpy as jnp
from jax import lax

SAMPLES = 7680
MARGIN = 256
BINS = 256
F0 = 16
LAGS = 256
LAG_STEP = 8
SRC = 16
ROUNDS = 3
RECORD = 7936
CHANNELS = 8192
WINDOWS = 12


def with_ends(array, own_key, low, high):
    place = [jax.random.randint(jax.random.fold_in(own_key, axis), (), 0, length) for axis, length in enumerate(array.shape)]
    longest = array.shape.index(max(array.shape))
    next_to = place[:longest] + [(place[longest] + 1) % array.shape[longest]] + place[longest + 1:]
    return array.at[tuple(place)].set(low).at[tuple(next_to)].set(high)


def block_scale(rng, extent, shards, smallest, largest):
    level = 1.0
    for position, blocks in shards:
        heights = jax.random.uniform(jax.random.fold_in(jax.random.fold_in(rng, 6), position), (blocks,), jnp.float32, smallest / len(shards), largest / len(shards))
        level = level * jnp.repeat(jnp.exp(heights), extent[position] // blocks).reshape((-1,) + (1,) * (len(extent) - 1 - position))
    return level


def noise(own_key, dims, scale, limit, cuts=(), kind=jnp.bfloat16):
    gain = block_scale(own_key, dims, cuts, -0.22, 0.18) if cuts else 1.0
    values = jax.random.normal(own_key, dims, jnp.float32) * scale * gain
    return jnp.minimum(jnp.maximum(values, -limit), limit).astype(kind)


def setup_inputs(seed: int = 0) -> dict:
    splits = jax.random.split(jax.random.key(seed), 4)
    return {
        "record": noise(splits[0], (WINDOWS, RECORD, CHANNELS), 1.0, 6.0, ((0, 4), (1, 32))),
        "offsets": with_ends(jax.random.randint(splits[1], (WINDOWS,), 0, MARGIN + 1), jax.random.fold_in(splits[1], 1), 0, MARGIN).astype(jnp.int32),
        "sources": with_ends(jax.random.randint(splits[2], (ROUNDS, SRC), 0, CHANNELS), jax.random.fold_in(splits[2], 1), 0, CHANNELS - 1).astype(jnp.int32),
    }


def dft_table():
    steps = jnp.arange(SAMPLES, dtype=jnp.int32)
    freqs = jnp.arange(BINS, dtype=jnp.int32) + F0
    phase = freqs[:, None] * steps[None, :] % SAMPLES
    angle = 2.0 * math.pi / SAMPLES * phase.astype(jnp.float32)
    taper = 0.5 - 0.5 * jnp.cos(2.0 * math.pi / SAMPLES * steps.astype(jnp.float32))
    rows = jnp.concatenate([taper[None, :] * jnp.cos(angle), -taper[None, :] * jnp.sin(angle)], axis=0)
    return rows.astype(jnp.bfloat16)

def lag_tables():
    lag_ids = jnp.arange(LAGS, dtype=jnp.int32)
    shifts = LAG_STEP * (lag_ids - LAGS // 2)
    freqs = jnp.arange(BINS, dtype=jnp.int32) + F0
    phase = shifts[:, None] * freqs[None, :] % SAMPLES
    angle = 2.0 * math.pi / SAMPLES * phase.astype(jnp.float32)
    return (jnp.cos(angle), jnp.sin(angle))

def make_kernel(chosen, scale):
    cos_lag, sin_lag = lag_tables()
    real_part = chosen[:, :BINS, :]
    imag_part = chosen[:, BINS:, :]
    high = lax.Precision.HIGHEST
    first = jnp.einsum('wfs,kf->skwf', real_part, cos_lag, precision=high) + jnp.einsum('wfs,kf->skwf', imag_part, sin_lag, precision=high)
    second = jnp.einsum('wfs,kf->skwf', imag_part, cos_lag, precision=high) - jnp.einsum('wfs,kf->skwf', real_part, sin_lag, precision=high)
    joined = jnp.concatenate([first, second], axis=3) * scale
    count = chosen.shape[2]
    return joined.reshape(count * LAGS, chosen.shape[0] * 2 * BINS).astype(jnp.bfloat16)

def reference(record, offsets, sources):
    table = dft_table()
    spectra = []
    for window in range(WINDOWS):
        segment = lax.dynamic_slice_in_dim(record[window], offsets[window].astype(jnp.int32), SAMPLES, 0)
        spectra.append(jnp.dot(table, segment, preferred_element_type=jnp.float32))
    spectra = jnp.stack(spectra, axis=0)
    power = lax.optimization_barrier(jnp.mean(spectra * spectra, axis=1, keepdims=True))
    white = (spectra * lax.rsqrt(power + 1e-06)).astype(jnp.bfloat16)
    flat = white.reshape(WINDOWS * 2 * BINS, CHANNELS)
    scale = 1.0 / math.sqrt(WINDOWS * BINS)
    results = []
    for step in range(ROUNDS):
        chosen = jnp.take(white, sources[step], axis=2).astype(jnp.float32)
        kernel = make_kernel(chosen, scale)
        joint = jnp.dot(kernel, flat, preferred_element_type=jnp.float32)
        results.append(joint.astype(jnp.bfloat16).reshape(SRC, LAGS, CHANNELS))
    return jnp.stack(results, axis=0)
```

```python
import math

import jax
import jax.numpy as jnp
import numpy as np
from jax import lax
from jax.sharding import PartitionSpec as P

SAMPLES = 7680
BINS = 256
F0 = 16
LAGS = 256
LAG_STEP = 8
ROUNDS = 3
RANK = 32
GROUPS = BINS // 8
SLOTS = 16


def sample_basis(count):
    half = (F0 + BINS) / SAMPLES
    at = np.arange(count)
    matrix = np.diag(((count - 1) / 2 - at) ** 2 * math.cos(2 * math.pi * half))
    side = at[1:] * (count - at[1:]) / 2
    matrix = matrix + np.diag(side, 1) + np.diag(side, -1)
    vectors = np.linalg.eigh(matrix)[1][:, ::-1][:, :RANK]
    return vectors * np.where(vectors[0] < 0, -1.0, 1.0)


def spectrum_tables(count, blocks):
    basis = sample_basis(count)
    middle = (count - 1) / 2
    at = np.arange(count) - middle
    terms = []
    for step, weight in ((0, 0.5), (1, -0.25), (-1, -0.25)):
        freqs = np.arange(BINS) + F0 + step
        wave = np.exp(-2j * math.pi / SAMPLES * np.outer(freqs, at)) @ basis
        turn = np.exp(-2j * math.pi / SAMPLES * np.outer(freqs, count * np.arange(blocks) + middle))
        terms.append(weight * (turn[:, :, None] * wave[:, None, :]).reshape(BINS, blocks * RANK))
    own, above, below = terms
    return np.stack([np.stack([t.real, t.imag]) for t in (own, above + below, above - below)]).astype(np.float32)


def lag_matrix(scale):
    shifts = LAG_STEP * (np.arange(LAGS) - LAGS // 2)
    phase = shifts[:, None] * (np.arange(BINS) + F0)[None, :] % SAMPLES
    angle = 2 * math.pi / SAMPLES * phase
    both = np.stack([np.cos(angle), np.sin(angle)], axis=1).reshape(LAGS, 2, GROUPS, 8)
    return (both.transpose(0, 2, 1, 3).reshape(LAGS, 2 * BINS) * scale).astype(np.float32)


def split_pair(array):
    high = array.astype(jnp.bfloat16)
    return high, (array - high.astype(jnp.float32)).astype(jnp.bfloat16)


def body(record, offsets, sources):
    windows, count, channels = record.shape
    blocks, hosts = lax.axis_size("chan"), lax.axis_size("win")
    width = channels // blocks
    first = lax.axis_index("chan") * count

    at = first + jnp.arange(count, dtype=jnp.int32)[None, :] - offsets[:, None]
    inside = (at >= 0) & (at < SAMPLES)
    basis = jnp.asarray(sample_basis(count).T.astype(np.float32))
    masked = jnp.where(inside[:, None, :], basis[None], 0.0)
    high, low = split_pair(masked)
    pair = jnp.concatenate([high, low], axis=1)
    coef = jnp.einsum("wrj,wjc->wrc", pair, record, preferred_element_type=jnp.float32)
    coef = (coef[:, :RANK] + coef[:, RANK:]).astype(jnp.bfloat16)

    per = sources.shape[1] // hosts
    wanted = sources.reshape(ROUNDS, hosts, per).transpose(1, 0, 2).reshape(hosts, ROUNDS * per)
    wanted = jnp.pad(wanted, ((0, 0), (0, SLOTS - ROUNDS * per)), constant_values=-1).reshape(-1)
    onehot = (jnp.arange(channels, dtype=jnp.int32)[:, None] == wanted[None, :]).astype(jnp.bfloat16)
    picked = jnp.einsum("wrc,cs->wrs", coef, onehot, preferred_element_type=jnp.float32).astype(jnp.bfloat16)

    cut = coef.reshape(windows, RANK, blocks, width).transpose(2, 0, 1, 3)
    extra = jnp.broadcast_to(picked[None], (blocks,) + picked.shape)
    sent = jnp.concatenate([cut, extra], axis=3)
    got = lax.all_to_all(sent, "chan", split_axis=0, concat_axis=0, tiled=True)
    got = got.transpose(1, 0, 2, 3).reshape(windows, blocks * RANK, -1)

    tables = jnp.asarray(spectrum_tables(count, blocks))
    freqs = jnp.arange(BINS, dtype=jnp.int32) + F0
    turn = 2 * math.pi / SAMPLES * (freqs[None, :] * offsets[:, None] % SAMPLES).astype(jnp.float32)
    step = 2 * math.pi / SAMPLES * offsets.astype(jnp.float32)
    white = []
    for w in range(windows):
        c, s = jnp.cos(step[w]), jnp.sin(step[w])
        re = tables[0, 0] + c * tables[1, 0] - s * tables[2, 1]
        im = tables[0, 1] + c * tables[1, 1] + s * tables[2, 0]
        c, s = jnp.cos(turn[w])[:, None], jnp.sin(turn[w])[:, None]
        full = jnp.stack([(c * re - s * im).reshape(GROUPS, 8, -1), (c * im + s * re).reshape(GROUPS, 8, -1)], axis=1)
        full = full.reshape(2 * BINS, -1).astype(jnp.bfloat16)
        spectra = jnp.dot(full, got[w], preferred_element_type=jnp.float32)
        power = jnp.mean(spectra * spectra, axis=0, keepdims=True)
        white.append((spectra * lax.rsqrt(power + 1e-06)).astype(jnp.bfloat16))
    white = jnp.stack(white)
    white = lax.all_gather(white, "win", axis=0, tiled=True)
    mine = lax.dynamic_slice_in_dim(white, width + SLOTS * lax.axis_index("win"), ROUNDS * per, 2)
    white = white[:, :, :width]

    total = windows * hosts
    count = ROUNDS * per
    white = white.reshape(total, GROUPS, 16, width).transpose(1, 0, 2, 3).reshape(GROUPS, total * 16, width)
    mine = mine.reshape(total, GROUPS, 2, 8, count)
    turned = jnp.stack([mine[:, :, 1], -mine[:, :, 0]], axis=2)
    rows = jnp.stack([mine, turned]).transpose(2, 5, 0, 1, 3, 4)
    eye = jnp.eye(8, dtype=jnp.bfloat16)
    spread = (rows[:, :, :, None] * eye[:, None, None, :]).reshape(GROUPS, count * 16, total * 16)
    cross = jnp.einsum("gmk,gkc->gmc", spread, white, preferred_element_type=jnp.float32).astype(jnp.bfloat16)
    cross = cross.reshape(GROUPS, count, 16, width).transpose(1, 0, 2, 3).reshape(count, 2 * BINS, width)
    lags = jnp.asarray(lag_matrix(1 / math.sqrt(total * BINS))).astype(jnp.bfloat16)
    out = jnp.einsum("kf,sfc->skc", lags, cross, preferred_element_type=jnp.float32)
    return out.astype(jnp.bfloat16).reshape(ROUNDS, per, LAGS, width)


def solution(mesh):
    return jax.shard_map(
        body,
        mesh=mesh,
        in_specs=(P("win", "chan", None), P("win"), P()),
        out_specs=P(None, "win", None, "chan"),
        check_vma=False,
    )
```

```python
import math

import jax
import jax.numpy as jnp
import numpy as np
from jax import lax
from jax.experimental import pallas as pl
from jax.experimental.pallas import tpu as pltpu
from jax.sharding import PartitionSpec as P

SAMPLES = 7680
BINS = 256
F0 = 16
LAGS = 256
LAG_STEP = 8
ROUNDS = 3
RANK = 32
GROUPS = BINS // 8
SLOTS = 16


def sample_basis(count):
    half = (F0 + BINS) / SAMPLES
    at = np.arange(count)
    matrix = np.diag(((count - 1) / 2 - at) ** 2 * math.cos(2 * math.pi * half))
    side = at[1:] * (count - at[1:]) / 2
    matrix = matrix + np.diag(side, 1) + np.diag(side, -1)
    vectors = np.linalg.eigh(matrix)[1][:, ::-1][:, :RANK]
    return vectors * np.where(vectors[0] < 0, -1.0, 1.0)


def spectrum_tables(count, blocks):
    basis = sample_basis(count)
    middle = (count - 1) / 2
    at = np.arange(count) - middle
    terms = []
    for step, weight in ((0, 0.5), (1, -0.25), (-1, -0.25)):
        freqs = np.arange(BINS) + F0 + step
        wave = np.exp(-2j * math.pi / SAMPLES * np.outer(freqs, at)) @ basis
        turn = np.exp(-2j * math.pi / SAMPLES * np.outer(freqs, count * np.arange(blocks) + middle))
        terms.append(weight * (turn[:, :, None] * wave[:, None, :]).reshape(BINS, blocks * RANK))
    own, above, below = terms
    return np.stack([np.stack([t.real, t.imag]) for t in (own, above + below, above - below)]).astype(np.float32)


def lag_matrix(scale):
    shifts = LAG_STEP * (np.arange(LAGS) - LAGS // 2)
    phase = shifts[:, None] * (np.arange(BINS) + F0)[None, :] % SAMPLES
    angle = 2 * math.pi / SAMPLES * phase
    both = np.stack([np.cos(angle), np.sin(angle)], axis=1).reshape(LAGS, 2, GROUPS, 8)
    return (both.transpose(0, 2, 1, 3).reshape(LAGS, 2 * BINS) * scale).astype(np.float32)


def split_pair(array):
    high = array.astype(jnp.bfloat16)
    return high, (array - high.astype(jnp.float32)).astype(jnp.bfloat16)


def correlate(white_ref, rows_ref, lag_ref, out_ref, cross):
    hosts, windows = white_ref.shape[:2]
    used = cross.shape[0]

    @pl.when(pl.program_id(0) == 0)
    def _():
        lane = lax.broadcasted_iota(jnp.int32, (SLOTS, 128), 1)
        left = lane < 64
        real = lane % 16 < 8
        own = lax.broadcasted_iota(jnp.int32, (8, 256), 1) % 8 == lax.broadcasted_iota(jnp.int32, (8, 256), 0)
        own = jnp.where(own, 1.0, 0.0).astype(jnp.float32)
        blank = jnp.zeros((16, white_ref.shape[4]), jnp.bfloat16)

        def pair(at, _):
            tiles = [rows_ref[j, at].astype(jnp.float32) for j in range(hosts)]
            for odd in range(2):
                halves, turned = [], []
                for j in range(0, hosts, 2):
                    if odd:
                        both = jnp.where(left, pltpu.roll(tiles[j], 64, 1), tiles[j + 1])
                    else:
                        both = jnp.where(left, tiles[j], pltpu.roll(tiles[j + 1], 64, 1))
                    halves.append(both)
                    turned.append(jnp.where(real, pltpu.roll(both, 120, 1), -pltpu.roll(both, 8, 1)))
                first = jnp.concatenate(halves, axis=1)[:used]
                second = jnp.concatenate(turned, axis=1)[:used]
                spread = jnp.stack([first[:, None, :] * own[None], second[:, None, :] * own[None]], axis=1)
                spread = spread.reshape(used * 16, 256).astype(jnp.bfloat16)
                group = at * 2 + odd
                parts = []
                for j in range(hosts):
                    parts += [white_ref[j, w, group] for w in range(windows)] + [blank]
                found = jnp.dot(spread, jnp.concatenate(parts, axis=0), preferred_element_type=jnp.float32)
                cross[:, group] = found.astype(jnp.bfloat16).reshape(used, 16, -1)
            return 0

        lax.fori_loop(0, GROUPS // 2, pair, 0)

    spectrum = cross[pl.program_id(0)].reshape(2 * BINS, -1)
    found = jnp.dot(lag_ref[...], spectrum, preferred_element_type=jnp.float32)
    out_ref[0] = (found[:LAGS] + found[LAGS:]).astype(jnp.bfloat16)


def correlations(white, rows, total, used):
    hosts, windows, _, _, width = white.shape
    lags = split_pair(jnp.asarray(lag_matrix(1 / math.sqrt(total * BINS))))
    return pl.pallas_call(
        correlate,
        grid=(used,),
        out_shape=jax.ShapeDtypeStruct((used, LAGS, width), jnp.bfloat16),
        in_specs=[
            pl.BlockSpec(white.shape, lambda s: (0,) * 5),
            pl.BlockSpec(rows.shape, lambda s: (0,) * 4),
            pl.BlockSpec((2 * LAGS, 2 * BINS), lambda s: (0, 0)),
        ],
        out_specs=pl.BlockSpec((1, LAGS, width), lambda s: (s, 0, 0)),
        scratch_shapes=[pltpu.VMEM((used, GROUPS, 16, width), jnp.bfloat16)],
        compiler_params=pltpu.CompilerParams(vmem_limit_bytes=32 << 20),
    )(white, rows, jnp.concatenate(lags, axis=0))


def body(record, offsets, sources):
    windows, count, channels = record.shape
    blocks, hosts = lax.axis_size("chan"), lax.axis_size("win")
    width = channels // blocks
    first = lax.axis_index("chan") * count

    at = first + jnp.arange(count, dtype=jnp.int32)[None, :] - offsets[:, None]
    inside = (at >= 0) & (at < SAMPLES)
    basis = jnp.asarray(sample_basis(count).T.astype(np.float32))
    masked = jnp.where(inside[:, None, :], basis[None], 0.0)
    high, low = split_pair(masked)
    pair = jnp.concatenate([high, low], axis=1)
    coef = jnp.einsum("wrj,wjc->wrc", pair, record, preferred_element_type=jnp.float32)
    coef = (coef[:, :RANK] + coef[:, RANK:]).astype(jnp.bfloat16)

    per = sources.shape[1] // hosts
    wanted = sources.reshape(ROUNDS, hosts, per).transpose(1, 0, 2).reshape(hosts, ROUNDS * per)
    wanted = jnp.pad(wanted, ((0, 0), (0, SLOTS - ROUNDS * per)), constant_values=-1).reshape(-1)
    onehot = (jnp.arange(channels, dtype=jnp.int32)[:, None] == wanted[None, :]).astype(jnp.bfloat16)
    picked = jnp.einsum("wrc,cs->wrs", coef, onehot, preferred_element_type=jnp.float32).astype(jnp.bfloat16)

    cut = coef.reshape(windows, RANK, blocks, width).transpose(2, 0, 1, 3)
    extra = jnp.broadcast_to(picked[None], (blocks,) + picked.shape)
    sent = jnp.concatenate([cut, extra], axis=3)
    got = lax.all_to_all(sent, "chan", split_axis=0, concat_axis=0, tiled=True)
    got = got.transpose(1, 0, 2, 3).reshape(windows, blocks * RANK, -1)

    tables = jnp.asarray(spectrum_tables(count, blocks))
    freqs = jnp.arange(BINS, dtype=jnp.int32) + F0
    turn = 2 * math.pi / SAMPLES * (freqs[None, :] * offsets[:, None] % SAMPLES).astype(jnp.float32)
    step = 2 * math.pi / SAMPLES * offsets.astype(jnp.float32)
    white = []
    for w in range(windows):
        c, s = jnp.cos(step[w]), jnp.sin(step[w])
        re = tables[0, 0] + c * tables[1, 0] - s * tables[2, 1]
        im = tables[0, 1] + c * tables[1, 1] + s * tables[2, 0]
        c, s = jnp.cos(turn[w])[:, None], jnp.sin(turn[w])[:, None]
        full = jnp.stack([(c * re - s * im).reshape(GROUPS, 8, -1), (c * im + s * re).reshape(GROUPS, 8, -1)], axis=1)
        full = full.reshape(2 * BINS, -1).astype(jnp.bfloat16)
        spectra = jnp.dot(full, got[w], preferred_element_type=jnp.float32)
        power = jnp.mean(spectra * spectra, axis=0, keepdims=True)
        white.append((spectra * lax.rsqrt(power + 1e-06)).astype(jnp.bfloat16))
    white = jnp.stack(white)
    rows = white[:, :, width:].reshape(windows, GROUPS, 16, -1)
    rows = jnp.pad(rows.transpose(3, 1, 0, 2), ((0, 0), (0, 0), (0, 64 // 16 - windows), (0, 0)))
    rows = rows.reshape(hosts, SLOTS, GROUPS // 2, 128).transpose(0, 2, 1, 3)
    white = lax.all_gather(white[:, :, :width].reshape(windows, GROUPS, 16, width), "win", axis=0)
    rows = lax.all_gather(rows, "win", axis=0)
    rows = lax.dynamic_index_in_dim(rows, lax.axis_index("win"), 1, keepdims=False)
    out = correlations(white, rows, windows * hosts, ROUNDS * per)
    return out.reshape(ROUNDS, per, LAGS, width)


def solution(mesh):
    return jax.shard_map(
        body,
        mesh=mesh,
        in_specs=(P("win", "chan", None), P("win"), P()),
        out_specs=P(None, "win", None, "chan"),
        check_vma=False,
    )
```

```python
import math

import jax
import jax.numpy as jnp
import numpy as np
from jax import lax
from jax.experimental import pallas as pl
from jax.experimental.pallas import tpu as pltpu
from jax.sharding import PartitionSpec as P

SAMPLES = 7680
BINS = 256
F0 = 16
LAGS = 256
LAG_STEP = 8
ROUNDS = 3
RANK = 32
GROUPS = BINS // 8
SLOTS = 16
MESH = pl.DeviceIdType.MESH


def sample_basis(count):
    half = (F0 + BINS) / SAMPLES
    at = np.arange(count)
    matrix = np.diag(((count - 1) / 2 - at) ** 2 * math.cos(2 * math.pi * half))
    side = at[1:] * (count - at[1:]) / 2
    matrix = matrix + np.diag(side, 1) + np.diag(side, -1)
    vectors = np.linalg.eigh(matrix)[1][:, ::-1][:, :RANK]
    return vectors * np.where(vectors[0] < 0, -1.0, 1.0)


def spectrum_tables(count, blocks):
    basis = sample_basis(count)
    middle = (count - 1) / 2
    at = np.arange(count) - middle
    terms = []
    for step, weight in ((0, 0.5), (1, -0.25), (-1, -0.25)):
        freqs = np.arange(BINS) + F0 + step
        wave = np.exp(-2j * math.pi / SAMPLES * np.outer(freqs, at)) @ basis
        turn = np.exp(-2j * math.pi / SAMPLES * np.outer(freqs, count * np.arange(blocks) + middle))
        table = weight * (turn[:, :, None] * wave[:, None, :]).reshape(BINS, blocks, 2, RANK // 2)
        terms.append(table.transpose(0, 2, 1, 3).reshape(BINS, blocks * RANK))
    own, above, below = terms
    return np.stack([p for t in (own, above + below, above - below) for p in (t.real, t.imag)]).astype(np.float32)


def lag_matrix(scale):
    shifts = LAG_STEP * (np.arange(LAGS) - LAGS // 2)
    phase = shifts[:, None] * (np.arange(BINS) + F0)[None, :] % SAMPLES
    angle = 2 * math.pi / SAMPLES * phase
    both = np.stack([np.cos(angle), np.sin(angle)], axis=1).reshape(LAGS, 2, GROUPS, 8)
    return (both.transpose(0, 2, 1, 3).reshape(LAGS, 2 * BINS) * scale).astype(np.float32)


def split_pair(array):
    high = array.astype(jnp.bfloat16)
    return high, (array - high.astype(jnp.float32)).astype(jnp.bfloat16)


def exchange(
    record, tables, basis, turns, picks, white_out, rows_out,
    held, parts, message, arrived, coded, full, spectra, columns, whites, rows,
    load_sem, table_sem, send_sem, recv_sem, pass_sem, take_sem, rows_send, rows_recv, own_sem,
):
    windows, chunks = held.shape[:2]
    blocks = message.shape[1]
    count = picks.shape[1]
    me, win = lax.axis_index("chan"), lax.axis_index("win")

    def load(w, k):
        at = (me // 4) ^ k
        source = record.at[w, :, pl.ds(pl.multiple_of(at * 1024, 1024), 1024)]
        return pltpu.make_async_copy(source, held.at[w, k], load_sem.at[w, k])

    def start_load(i, _):
        load(i // chunks, i % chunks).start()
        return 0

    lax.fori_loop(0, windows * chunks, start_load, 0)
    table_copy = pltpu.make_async_copy(tables, parts, table_sem)
    table_copy.start()

    barrier = pltpu.get_barrier_semaphore()

    def greet(k, _):
        pl.semaphore_signal(barrier, inc=1, device_id=(win, me ^ k), device_id_type=MESH)
        return 0

    lax.fori_loop(1, blocks, greet, 0)
    for k in (1, 2, 3):
        pl.semaphore_signal(barrier, inc=1, device_id=(win ^ k, me), device_id_type=MESH)

    lane = lax.broadcasted_iota(jnp.int32, (16, 128), 1)
    columns[:, 48:, :] = jnp.zeros((GROUPS, 16, 128), jnp.float32)

    def project(w):
        def chunk(k, _):
            load(w, k).wait()
            at = (me // 4) ^ k
            found = jnp.dot(basis[w], held[w, k], preferred_element_type=jnp.float32)
            found = (found[:RANK] + found[RANK:]).astype(jnp.bfloat16)
            for i in range(4):
                part = found[:, 256 * i : 256 * (i + 1)]
                message[w, at * 4 + i, :, 0:256] = part[:16]
                message[w, at * 4 + i, :, 256:512] = part[16:]
            for i in range(8):
                coded[at * 8 + i] = found[:, 128 * i : 128 * (i + 1)]
            return 0

        lax.fori_loop(0, chunks, chunk, 0)

        def pick(i, total):
            tile = coded[picks[0, i]].astype(jnp.float32)
            wide = lax.broadcasted_iota(jnp.int32, (RANK, 128), 1)
            value = jnp.sum(jnp.where(wide == picks[1, i], tile, 0.0), axis=1, keepdims=True)
            slot = i // 12 * SLOTS + i % 12
            total = jnp.where(lane == slot, value[:16], total)
            return jnp.where(lane == slot + 64, value[16:], total)

        chosen = lax.fori_loop(0, count, pick, jnp.zeros((16, 128), jnp.float32)).astype(jnp.bfloat16)

        def fill(c, _):
            message[w, c, :, 512:640] = chosen
            return 0

        lax.fori_loop(0, blocks, fill, 0)
        arrived[w, me] = message[w, me]

    def send(w, k):
        return pltpu.make_async_remote_copy(
            message.at[w, me ^ k], arrived.at[w, me], send_sem.at[w, k], recv_sem.at[w, me],
            device_id=(win, me ^ k), device_id_type=MESH,
        )

    def receive(w, k):
        return pltpu.make_async_remote_copy(
            message.at[w, me ^ k], arrived.at[w, me ^ k], send_sem.at[w, k], recv_sem.at[w, me ^ k],
            device_id=(win, me ^ k), device_id_type=MESH,
        )

    def start_sends(w):
        def one(k, _):
            send(w, k).start()
            return 0

        lax.fori_loop(1, blocks, one, 0)

    project(0)
    pl.semaphore_wait(barrier, blocks - 1 + 3)
    start_sends(0)

    def later(w, _):
        project(w)
        start_sends(w)
        return 0

    lax.fori_loop(1, windows, later, 0)

    table_copy.wait()

    def tabulate(i, _):
        w, g = i // GROUPS, i % GROUPS
        own_re, own_im, sum_re, sum_im, dif_re, dif_im = [parts[t, pl.ds(pl.multiple_of(g * 8, 8), 8)] for t in range(6)]
        turn = turns[w, pl.ds(pl.multiple_of(g * 8, 8), 8)]
        c, s = turn[:, 2:3], turn[:, 3:4]
        re = own_re + c * sum_re - s * dif_im
        im = own_im + c * sum_im + s * dif_re
        c, s = turn[:, 0:1], turn[:, 1:2]
        both = jnp.concatenate([c * re - s * im, c * im + s * re], axis=0)
        high = both.astype(jnp.bfloat16)
        full[w, 0, g] = high
        full[w, 1, g] = (both - high.astype(jnp.float32)).astype(jnp.bfloat16)
        return 0

    lax.fori_loop(0, windows * GROUPS, tabulate, 0)

    def hand(w, k):
        return pltpu.make_async_remote_copy(
            whites.at[w], white_out.at[win, w], pass_sem.at[k - 1, w], take_sem.at[k - 1, w],
            device_id=(win ^ k, me), device_id_type=MESH,
        )

    def taken(w, k):
        return pltpu.make_async_remote_copy(
            whites.at[w], white_out.at[win ^ k, w], pass_sem.at[k - 1, w], take_sem.at[k - 1, w],
            device_id=(win ^ k, me), device_id_type=MESH,
        )

    def relay(w, owner):
        return pltpu.make_async_remote_copy(
            white_out.at[owner, w], white_out.at[owner, w], pass_sem.at[2, w], take_sem.at[2, w],
            device_id=(win ^ 1, me), device_id_type=MESH,
        )

    def keep(w):
        return pltpu.make_async_copy(whites.at[w], white_out.at[win, w], own_sem.at[w])

    def whiten(w, _):
        def wait_one(k, _):
            receive(w, k).wait_recv()
            return 0

        lax.fori_loop(1, blocks, wait_one, 0)
        first = arrived[w, :, :, 0:256].reshape(blocks * 16, 256)
        second = arrived[w, :, :, 256:512].reshape(blocks * 16, 256)
        extra = arrived[w, :, :, 512:640].reshape(blocks * 16, 128)
        cut = blocks * 16

        def tile(m, power):
            found = jnp.zeros((128, 256), jnp.float32)
            low = jnp.zeros((128, 128), jnp.float32)
            top = jnp.zeros((128, 128), jnp.float32)
            for half in range(2):
                table = full[w, half, pl.ds(m * 8, 8)].reshape(128, 2 * cut)
                left, right = table[:, :cut], table[:, cut:]
                found += jnp.dot(left, first, preferred_element_type=jnp.float32)
                found += jnp.dot(right, second, preferred_element_type=jnp.float32)
                low += jnp.dot(left, extra, preferred_element_type=jnp.float32)
                top += jnp.dot(right, extra, preferred_element_type=jnp.float32)
            rows_at = pl.ds(pl.multiple_of(m * 128, 128), 128)
            spectra[rows_at, 0:256] = found
            mine = low + pltpu.roll(top, 64, 1)
            spectra[rows_at, 256:384] = mine
            return power[0] + jnp.sum(found * found, axis=0, keepdims=True), power[1] + jnp.sum(mine * mine, axis=0, keepdims=True)

        zero = jnp.zeros((1, 256), jnp.float32), jnp.zeros((1, 128), jnp.float32)
        power = lax.fori_loop(0, 4, tile, zero)
        scale, scale_picked = [lax.rsqrt(p * (1 / (2 * BINS)) + 1e-06) for p in power]

        def norm(m, _):
            rows_at = pl.ds(pl.multiple_of(m * 128, 128), 128)
            white = (spectra[rows_at, 0:256] * scale).astype(jnp.bfloat16)
            whites[w, pl.ds(m * 8, 8)] = white.reshape(8, 16, 256)
            white = (spectra[rows_at, 256:384] * scale_picked).astype(jnp.bfloat16).astype(jnp.float32)
            columns[pl.ds(m * 8, 8), pl.ds(pl.multiple_of(w * 16, 16), 16)] = white.reshape(8, 16, 128)
            return 0

        lax.fori_loop(0, 4, norm, 0)
        hand(w, 2).start()
        hand(w, 1).start()
        keep(w).start()
        return 0

    lax.fori_loop(0, windows, whiten, 0)

    def turn_over(at, _):
        block = columns[pl.ds(at * 2, 2)].reshape(128, 128).T
        rows[:, at] = block[:64].reshape(4, SLOTS, 128).astype(jnp.bfloat16)
        return 0

    lax.fori_loop(0, GROUPS // 2, turn_over, 0)

    def deal(k):
        return pltpu.make_async_remote_copy(
            rows.at[win ^ k], rows_out.at[win], rows_send.at[k], rows_recv.at[k],
            device_id=(win ^ k, me), device_id_type=MESH,
        )

    def dealt(k):
        return pltpu.make_async_remote_copy(
            rows.at[win ^ k], rows_out.at[win ^ k], rows_send.at[k], rows_recv.at[k],
            device_id=(win ^ k, me), device_id_type=MESH,
        )

    for k in (3, 2, 1):
        deal(k).start()
    own_rows = pltpu.make_async_copy(rows.at[win], rows_out.at[win], rows_send.at[0])
    own_rows.start()

    def forward(w, _):
        taken(w, 2).wait_recv()
        relay(w, win ^ 2).start()
        return 0

    lax.fori_loop(0, windows, forward, 0)

    def finish(w, _):
        keep(w).wait()
        hand(w, 1).wait_send()
        hand(w, 2).wait_send()
        taken(w, 1).wait_recv()
        relay(w, win ^ 2).wait_send()
        relay(w, win ^ 3).wait_recv()

        def sent(k, _):
            send(w, k).wait_send()
            return 0

        lax.fori_loop(1, blocks, sent, 0)
        return 0

    lax.fori_loop(0, windows, finish, 0)
    own_rows.wait()
    for k in (1, 2, 3):
        deal(k).wait_send()
        dealt(k).wait_recv()


def exchanged(record, tables, basis, turns, picks, blocks, hosts):
    windows, count, channels = record.shape
    width = channels // blocks
    dma = pltpu.SemaphoreType.DMA
    anywhere = pl.BlockSpec(memory_space=pl.ANY)
    return pl.pallas_call(
        exchange,
        out_shape=(
            jax.ShapeDtypeStruct((hosts, windows, GROUPS, 16, width), jnp.bfloat16),
            jax.ShapeDtypeStruct((hosts, GROUPS // 2, SLOTS, 128), jnp.bfloat16),
        ),
        in_specs=[
            anywhere,
            anywhere,
            pl.BlockSpec(memory_space=pltpu.VMEM),
            pl.BlockSpec(memory_space=pltpu.VMEM),
            pl.BlockSpec(memory_space=pltpu.SMEM),
        ],
        out_specs=(anywhere, anywhere),
        scratch_shapes=[
            pltpu.VMEM((windows, 8, count, channels // 8), jnp.bfloat16),
            pltpu.VMEM(tables.shape, jnp.float32),
            pltpu.VMEM((windows, blocks, 16, 640), jnp.bfloat16),
            pltpu.VMEM((windows, blocks, 16, 640), jnp.bfloat16),
            pltpu.VMEM((channels // 128, RANK, 128), jnp.bfloat16),
            pltpu.VMEM((windows, 2, GROUPS, 16, blocks * RANK), jnp.bfloat16),
            pltpu.VMEM((2 * BINS, 384), jnp.float32),
            pltpu.VMEM((GROUPS, 64, 128), jnp.float32),
            pltpu.VMEM((windows, GROUPS, 16, width), jnp.bfloat16),
            pltpu.VMEM((hosts, GROUPS // 2, SLOTS, 128), jnp.bfloat16),
            dma((windows, 8)),
            dma,
            dma((windows, blocks)),
            dma((windows, blocks)),
            dma((3, windows)),
            dma((3, windows)),
            dma((4,)),
            dma((4,)),
            dma((windows,)),
        ],
        compiler_params=pltpu.CompilerParams(collective_id=0, has_side_effects=True, vmem_limit_bytes=48 << 20),
    )(record, tables, basis, turns, picks)


def correlate(white_ref, rows_ref, lag_ref, out_ref, cross):
    hosts, windows = white_ref.shape[:2]
    used = cross.shape[0]

    @pl.when(pl.program_id(0) == 0)
    def _():
        lane = lax.broadcasted_iota(jnp.int32, (SLOTS, 128), 1)
        left = lane < 64
        real = lane % 16 < 8
        own = lax.broadcasted_iota(jnp.int32, (8, 256), 1) % 8 == lax.broadcasted_iota(jnp.int32, (8, 256), 0)
        own = jnp.where(own, 1.0, 0.0).astype(jnp.float32)
        blank = jnp.zeros((16, white_ref.shape[4]), jnp.bfloat16)

        def pair(at, _):
            tiles = [rows_ref[j, at].astype(jnp.float32) for j in range(hosts)]
            for odd in range(2):
                halves, turned = [], []
                for j in range(0, hosts, 2):
                    if odd:
                        both = jnp.where(left, pltpu.roll(tiles[j], 64, 1), tiles[j + 1])
                    else:
                        both = jnp.where(left, tiles[j], pltpu.roll(tiles[j + 1], 64, 1))
                    halves.append(both)
                    turned.append(jnp.where(real, pltpu.roll(both, 120, 1), -pltpu.roll(both, 8, 1)))
                first = jnp.concatenate(halves, axis=1)[:used]
                second = jnp.concatenate(turned, axis=1)[:used]
                spread = jnp.stack([first[:, None, :] * own[None], second[:, None, :] * own[None]], axis=1)
                spread = spread.reshape(used * 16, 256).astype(jnp.bfloat16)
                group = at * 2 + odd
                parts = []
                for j in range(hosts):
                    parts += [white_ref[j, w, group] for w in range(windows)] + [blank]
                found = jnp.dot(spread, jnp.concatenate(parts, axis=0), preferred_element_type=jnp.float32)
                cross[:, group] = found.astype(jnp.bfloat16).reshape(used, 16, -1)
            return 0

        lax.fori_loop(0, GROUPS // 2, pair, 0)

    spectrum = cross[pl.program_id(0)].reshape(2 * BINS, -1)
    found = jnp.dot(lag_ref[...], spectrum, preferred_element_type=jnp.float32)
    out_ref[0] = (found[:LAGS] + found[LAGS:]).astype(jnp.bfloat16)


def correlations(white, rows, total, used):
    hosts, windows, _, _, width = white.shape
    lags = split_pair(jnp.asarray(lag_matrix(1 / math.sqrt(total * BINS))))
    return pl.pallas_call(
        correlate,
        grid=(used,),
        out_shape=jax.ShapeDtypeStruct((used, LAGS, width), jnp.bfloat16),
        in_specs=[
            pl.BlockSpec(white.shape, lambda s: (0,) * 5),
            pl.BlockSpec(rows.shape, lambda s: (0,) * 4),
            pl.BlockSpec((2 * LAGS, 2 * BINS), lambda s: (0, 0)),
        ],
        out_specs=pl.BlockSpec((1, LAGS, width), lambda s: (s, 0, 0)),
        scratch_shapes=[pltpu.VMEM((used, GROUPS, 16, width), jnp.bfloat16)],
        compiler_params=pltpu.CompilerParams(vmem_limit_bytes=32 << 20),
    )(white, rows, jnp.concatenate(lags, axis=0))


def body(record, offsets, sources):
    windows, count, channels = record.shape
    blocks, hosts = lax.axis_size("chan"), lax.axis_size("win")
    width = channels // blocks
    first = lax.axis_index("chan") * count

    at = first + jnp.arange(count, dtype=jnp.int32)[None, :] - offsets[:, None]
    inside = (at >= 0) & (at < SAMPLES)
    basis = sample_basis(count).T.astype(np.float32)
    high = basis.astype(jnp.bfloat16)
    low = (basis - high.astype(np.float32)).astype(jnp.bfloat16)
    basis = jnp.where(inside[:, None, :], jnp.asarray(np.concatenate([high, low]))[None], 0.0)

    per = sources.shape[1] // hosts
    wanted = sources.reshape(ROUNDS, hosts, per).transpose(1, 0, 2).reshape(-1)
    picks = jnp.stack([wanted // 128, wanted % 128])

    freqs = jnp.arange(BINS, dtype=jnp.int32) + F0
    turn = 2 * math.pi / SAMPLES * (freqs[None, :] * offsets[:, None] % SAMPLES).astype(jnp.float32)
    step = jnp.broadcast_to(2 * math.pi / SAMPLES * offsets.astype(jnp.float32)[:, None], turn.shape)
    turns = jnp.stack([jnp.cos(turn), jnp.sin(turn), jnp.cos(step), jnp.sin(step)], axis=2)
    turns = jnp.pad(turns, ((0, 0), (0, 0), (0, 124)))

    tables = jnp.asarray(spectrum_tables(count, blocks))
    white, rows = exchanged(record, tables, basis, turns, picks, blocks, hosts)
    out = correlations(white, rows, windows * hosts, ROUNDS * per)
    return out.reshape(ROUNDS, per, LAGS, width)


def solution(mesh):
    return jax.shard_map(
        body,
        mesh=mesh,
        in_specs=(P("win", "chan", None), P("win"), P()),
        out_specs=P(None, "win", None, "chan"),
        check_vma=False,
    )
```

```python
import math

import jax
import jax.numpy as jnp
import numpy as np
from jax import lax
from jax.experimental import pallas as pl
from jax.experimental.pallas import tpu as pltpu
from jax.sharding import PartitionSpec as P

SAMPLES = 7680
BINS = 256
F0 = 16
LAGS = 256
LAG_STEP = 8
ROUNDS = 3
RANK = 32
GROUPS = BINS // 8
SLOTS = 16
MESH = pl.DeviceIdType.MESH


def sample_basis(count):
    half = (F0 + BINS) / SAMPLES
    at = np.arange(count)
    matrix = np.diag(((count - 1) / 2 - at) ** 2 * math.cos(2 * math.pi * half))
    side = at[1:] * (count - at[1:]) / 2
    matrix = matrix + np.diag(side, 1) + np.diag(side, -1)
    vectors = np.linalg.eigh(matrix)[1][:, ::-1][:, :RANK]
    return vectors * np.where(vectors[0] < 0, -1.0, 1.0)


def spectrum_tables(count, blocks):
    basis = sample_basis(count)
    middle = (count - 1) / 2
    at = np.arange(count) - middle
    terms = []
    for step, weight in ((0, 0.5), (1, -0.25), (-1, -0.25)):
        freqs = np.arange(BINS) + F0 + step
        wave = np.exp(-2j * math.pi / SAMPLES * np.outer(freqs, at)) @ basis
        turn = np.exp(-2j * math.pi / SAMPLES * np.outer(freqs, count * np.arange(blocks) + middle))
        table = weight * (turn[:, :, None] * wave[:, None, :]).reshape(BINS, blocks, 2, RANK // 2)
        terms.append(table.transpose(0, 2, 1, 3).reshape(BINS, blocks * RANK))
    own, above, below = terms
    return np.stack([p for t in (own, above + below, above - below) for p in (t.real, t.imag)]).astype(np.float32)


def lag_matrix(scale):
    shifts = LAG_STEP * (np.arange(LAGS) - LAGS // 2)
    phase = shifts[:, None] * (np.arange(BINS) + F0)[None, :] % SAMPLES
    angle = 2 * math.pi / SAMPLES * phase
    both = np.stack([np.cos(angle), np.sin(angle)], axis=1).reshape(LAGS, 2, GROUPS, 8)
    return (both.transpose(0, 2, 1, 3).reshape(LAGS, 2 * BINS) * scale).astype(np.float32)


def split_pair(array):
    high = array.astype(jnp.bfloat16)
    return high, (array - high.astype(array.dtype)).astype(jnp.bfloat16)


def exchange(
    record, tables, basis, offsets, sources, white_out, rows_out,
    held, parts, masked, turns, message, arrived, coded, picked, full, spectra, columns, whites, rows,
    load_sem, table_sem, send_sem, recv_sem, pass_sem, take_sem, rows_send, rows_recv, own_sem, pick_send, pick_recv,
):
    windows, chunks = held.shape[:2]
    blocks = message.shape[1]
    samples = held.shape[2]
    slots = sources.shape[1] // 4
    me, win = lax.axis_index("chan"), lax.axis_index("win")

    def load(w, k):
        at = (me // 4) ^ k
        source = record.at[w, :, pl.ds(pl.multiple_of(at * 1024, 1024), 1024)]
        return pltpu.make_async_copy(source, held.at[w, k], load_sem.at[w, k])

    def start_load(i, _):
        load(i // chunks, i % chunks).start()
        return 0

    lax.fori_loop(0, windows * chunks, start_load, 0)
    table_copy = pltpu.make_async_copy(tables, parts, table_sem)
    table_copy.start()

    barrier = pltpu.get_barrier_semaphore()

    def greet(k, _):
        pl.semaphore_signal(barrier, inc=1, device_id=(win, me ^ k), device_id_type=MESH)
        return 0

    lax.fori_loop(1, blocks, greet, 0)
    for k in (1, 2, 3):
        pl.semaphore_signal(barrier, inc=1, device_id=(win ^ k, me), device_id_type=MESH)

    for w in range(windows):
        time = lax.broadcasted_iota(jnp.int32, basis.shape, 1) + (me * samples - offsets[w])
        inside = (time >= 0) & (time < SAMPLES)
        masked[w] = jnp.where(inside, basis[...].astype(jnp.float32), 0.0).astype(jnp.bfloat16)

    wide = lax.broadcasted_iota(jnp.int32, turns.shape, 1)
    freq = jnp.where(wide % 4 < 2, lax.broadcasted_iota(jnp.int32, turns.shape, 0) + F0, 1)
    shift = jnp.zeros(turns.shape, jnp.int32)
    for w in range(windows):
        shift = jnp.where(wide // 4 == w, offsets[w], shift)
    turn = (freq * shift).astype(jnp.float32)
    turn = turn - SAMPLES * jnp.floor(turn * (1 / SAMPLES))
    turn = turn * (2 * math.pi / SAMPLES) - jnp.where(wide % 2 == 1, math.pi / 2, 0.0)
    turns[...] = jnp.cos(turn)

    lane = lax.broadcasted_iota(jnp.int32, (16, 128), 1)
    columns[:, 48:, :] = jnp.zeros((GROUPS, 16, 128), jnp.float32)

    def project(w):
        def chunk(k, _):
            load(w, k).wait()
            at = (me // 4) ^ k
            found = jnp.dot(masked[w], held[w, k], preferred_element_type=jnp.float32)
            found = (found[:RANK] + found[RANK:]).astype(jnp.bfloat16)
            for i in range(4):
                part = found[:, 256 * i : 256 * (i + 1)]
                message[w, at * 4 + i, :, 0:256] = part[:16]
                message[w, at * 4 + i, :, 256:512] = part[16:]
            for i in range(8):
                coded[w, at * 8 + i] = found[:, 128 * i : 128 * (i + 1)]
            return 0

        lax.fori_loop(0, chunks, chunk, 0)

        arrived[w, me] = message[w, me]

    def choose(w):
        wide = lax.broadcasted_iota(jnp.int32, (RANK, 128), 1)

        def pick(i, total):
            slot = i // 12 * SLOTS + i % 12
            source = sources[i % 12 // slots, i // 12 * slots + i % slots]
            tile = coded[w, source // 128].astype(jnp.float32)
            value = jnp.sum(jnp.where(wide == source % 128, tile, 0.0), axis=1, keepdims=True)
            total = jnp.where(lane == slot, value[:16], total)
            return jnp.where(lane == slot + 64, value[16:], total)

        chosen = lax.fori_loop(0, ROUNDS * slots * 4, pick, jnp.zeros((16, 128), jnp.float32), unroll=8)
        picked[me // 8, me // 4 % 2, me % 4, w] = chosen.astype(jnp.bfloat16)

    def cast(step, k):
        x, z, y = me // 8, me // 4 % 2, me % 4
        part = (picked.at[x, z, y], picked.at[x, :, y], picked.at[:, :, y])[step]
        return pltpu.make_async_remote_copy(
            part, part, pick_send.at[step, k], pick_recv.at[step, k],
            device_id=(win, me ^ (4, 8 * k, k)[step]), device_id_type=MESH,
        )

    def caught(step, k):
        there = me ^ (4, 8 * k, k)[step]
        x, z, y = there // 8, there // 4 % 2, there % 4
        part = (picked.at[x, z, y], picked.at[x, :, y], picked.at[:, :, y])[step]
        return pltpu.make_async_remote_copy(
            part, part, pick_send.at[step, k], pick_recv.at[step, k],
            device_id=(win, there), device_id_type=MESH,
        )

    def send(w, k):
        return pltpu.make_async_remote_copy(
            message.at[w, me ^ k], arrived.at[w, me], send_sem.at[w, k], recv_sem.at[w, me],
            device_id=(win, me ^ k), device_id_type=MESH,
        )

    def receive(w, k):
        return pltpu.make_async_remote_copy(
            message.at[w, me ^ k], arrived.at[w, me ^ k], send_sem.at[w, k], recv_sem.at[w, me ^ k],
            device_id=(win, me ^ k), device_id_type=MESH,
        )

    def start_sends(w):
        def one(k, _):
            send(w, k).start()
            return 0

        lax.fori_loop(1, blocks, one, 0)

    project(0)
    pl.semaphore_wait(barrier, blocks - 1 + 3)
    start_sends(0)
    project(1)
    start_sends(1)
    project(2)
    start_sends(2)
    choose(0)

    def later(w, _):
        choose(w)
        return 0

    lax.fori_loop(1, windows, later, 0)
    cast(0, 1).start()

    table_copy.wait()

    def tabulate(w, g):
        own_re, own_im, sum_re, sum_im, dif_re, dif_im = [parts[t, pl.ds(pl.multiple_of(g * 8, 8), 8)] for t in range(6)]
        turn = turns[pl.ds(pl.multiple_of(g * 8, 8), 8), :][:, 4 * w : 4 * w + 4]
        c, s = turn[:, 2:3], turn[:, 3:4]
        re = own_re + c * sum_re - s * dif_im
        im = own_im + c * sum_im + s * dif_re
        c, s = turn[:, 0:1], turn[:, 1:2]
        both = jnp.concatenate([c * re - s * im, c * im + s * re], axis=0)
        high = both.astype(jnp.bfloat16)
        full[w, 0, g] = high
        full[w, 1, g] = (both - high.astype(jnp.float32)).astype(jnp.bfloat16)
        return 0

    for w in range(windows):
        lax.fori_loop(0, GROUPS, lambda g, _, w=w: tabulate(w, g), 0, unroll=2)

    def hand(w, k):
        return pltpu.make_async_remote_copy(
            whites.at[w], white_out.at[win, w], pass_sem.at[k - 1, w], take_sem.at[k - 1, w],
            device_id=(win ^ k, me), device_id_type=MESH,
        )

    def taken(w, k):
        return pltpu.make_async_remote_copy(
            whites.at[w], white_out.at[win ^ k, w], pass_sem.at[k - 1, w], take_sem.at[k - 1, w],
            device_id=(win ^ k, me), device_id_type=MESH,
        )

    def relay(w, owner):
        return pltpu.make_async_remote_copy(
            white_out.at[owner, w], white_out.at[owner, w], pass_sem.at[2, w], take_sem.at[2, w],
            device_id=(win ^ 1, me), device_id_type=MESH,
        )

    def keep(w):
        return pltpu.make_async_copy(whites.at[w], white_out.at[win, w], own_sem.at[w])

    def whiten(w):
        def wait_one(k, _):
            receive(w, k).wait_recv()
            return 0

        lax.fori_loop(1, blocks, wait_one, 0)
        first = arrived[w, :, :, 0:256].reshape(blocks * 16, 256)
        second = arrived[w, :, :, 256:512].reshape(blocks * 16, 256)
        cut = blocks * 16

        def tile(m, power):
            found = jnp.zeros((128, 256), jnp.float32)
            for half in range(2):
                table = full[w, half, pl.ds(m * 8, 8)].reshape(128, 2 * cut)
                found += jnp.dot(table[:, :cut], first, preferred_element_type=jnp.float32)
                found += jnp.dot(table[:, cut:], second, preferred_element_type=jnp.float32)
            spectra[pl.ds(pl.multiple_of(m * 128, 128), 128)] = found
            return power + jnp.sum(found * found, axis=0, keepdims=True)

        power = lax.fori_loop(0, 4, tile, jnp.zeros((1, 256), jnp.float32))
        scale = lax.rsqrt(power * (1 / (2 * BINS)) + 1e-06)

        def norm(m, _):
            white = (spectra[pl.ds(pl.multiple_of(m * 128, 128), 128)] * scale).astype(jnp.bfloat16)
            whites[w, pl.ds(m * 8, 8)] = white.reshape(8, 16, 256)
            return 0

        lax.fori_loop(0, 4, norm, 0)
        hand(w, 2).start()
        hand(w, 1).start()
        keep(w).start()

    def whiten_picked(w, _):
        extra = picked[:, :, :, w].reshape(blocks * 16, 128)
        cut = blocks * 16

        def tile(m, power):
            low = jnp.zeros((128, 128), jnp.float32)
            top = jnp.zeros((128, 128), jnp.float32)
            for half in range(2):
                table = full[w, half, pl.ds(m * 8, 8)].reshape(128, 2 * cut)
                low += jnp.dot(table[:, :cut], extra, preferred_element_type=jnp.float32)
                top += jnp.dot(table[:, cut:], extra, preferred_element_type=jnp.float32)
            found = low + pltpu.roll(top, 64, 1)
            spectra[pl.ds(pl.multiple_of(m * 128, 128), 128), 0:128] = found
            return power + jnp.sum(found * found, axis=0, keepdims=True)

        power = lax.fori_loop(0, 4, tile, jnp.zeros((1, 128), jnp.float32))
        scale = lax.rsqrt(power * (1 / (2 * BINS)) + 1e-06)

        def norm(m, _):
            white = spectra[pl.ds(pl.multiple_of(m * 128, 128), 128), 0:128] * scale
            columns[pl.ds(m * 8, 8), pl.ds(pl.multiple_of(w * 16, 16), 16)] = (
                white.astype(jnp.bfloat16).astype(jnp.float32).reshape(8, 16, 128)
            )
            return 0

        lax.fori_loop(0, 4, norm, 0)
        return 0

    caught(0, 1).wait_recv()
    for k in (2, 1, 3):
        cast(1, k).start()
    whiten(0)
    for k in (1, 2, 3):
        caught(1, k).wait_recv()
    for k in (2, 1, 3):
        cast(2, k).start()
    whiten(1)
    whiten(2)
    for k in (1, 2, 3):
        caught(2, k).wait_recv()
    lax.fori_loop(0, windows, whiten_picked, 0)

    def turn_over(at, _):
        block = columns[pl.ds(at * 2, 2)].reshape(128, 128).T
        rows[:, at] = block[:64].reshape(4, SLOTS, 128).astype(jnp.bfloat16)
        return 0

    lax.fori_loop(0, GROUPS // 2, turn_over, 0)

    def deal(k):
        return pltpu.make_async_remote_copy(
            rows.at[win ^ k], rows_out.at[win], rows_send.at[k], rows_recv.at[k],
            device_id=(win ^ k, me), device_id_type=MESH,
        )

    def dealt(k):
        return pltpu.make_async_remote_copy(
            rows.at[win ^ k], rows_out.at[win ^ k], rows_send.at[k], rows_recv.at[k],
            device_id=(win ^ k, me), device_id_type=MESH,
        )

    for k in (3, 2, 1):
        deal(k).start()
    own_rows = pltpu.make_async_copy(rows.at[win], rows_out.at[win], rows_send.at[0])
    own_rows.start()

    def forward(w, _):
        taken(w, 2).wait_recv()
        relay(w, win ^ 2).start()
        return 0

    lax.fori_loop(0, windows, forward, 0)

    def finish(w, _):
        keep(w).wait()
        hand(w, 1).wait_send()
        hand(w, 2).wait_send()
        taken(w, 1).wait_recv()
        relay(w, win ^ 2).wait_send()
        relay(w, win ^ 3).wait_recv()

        def sent(k, _):
            send(w, k).wait_send()
            return 0

        lax.fori_loop(1, blocks, sent, 0)
        return 0

    lax.fori_loop(0, windows, finish, 0)
    own_rows.wait()
    cast(0, 1).wait_send()
    for k in (1, 2, 3):
        cast(1, k).wait_send()
        cast(2, k).wait_send()
        deal(k).wait_send()
        dealt(k).wait_recv()


def exchanged(record, tables, basis, offsets, sources, blocks, hosts):
    windows, count, channels = record.shape
    width = channels // blocks
    dma = pltpu.SemaphoreType.DMA
    anywhere = pl.BlockSpec(memory_space=pl.ANY)
    return pl.pallas_call(
        exchange,
        out_shape=(
            jax.ShapeDtypeStruct((hosts, windows, GROUPS, 16, width), jnp.bfloat16),
            jax.ShapeDtypeStruct((hosts, GROUPS // 2, SLOTS, 128), jnp.bfloat16),
        ),
        in_specs=[
            anywhere,
            anywhere,
            pl.BlockSpec(memory_space=pltpu.VMEM),
            pl.BlockSpec(memory_space=pltpu.SMEM),
            pl.BlockSpec(memory_space=pltpu.SMEM),
        ],
        out_specs=(anywhere, anywhere),
        scratch_shapes=[
            pltpu.VMEM((windows, 8, count, channels // 8), jnp.bfloat16),
            pltpu.VMEM(tables.shape, jnp.float32),
            pltpu.VMEM((windows,) + basis.shape, jnp.bfloat16),
            pltpu.VMEM((BINS, 128), jnp.float32),
            pltpu.VMEM((windows, blocks, 16, 2 * width), jnp.bfloat16),
            pltpu.VMEM((windows, blocks, 16, 2 * width), jnp.bfloat16),
            pltpu.VMEM((windows, channels // 128, RANK, 128), jnp.bfloat16),
            pltpu.VMEM((4, 2, 4, windows, 16, 128), jnp.bfloat16),
            pltpu.VMEM((windows, 2, GROUPS, 16, blocks * RANK), jnp.bfloat16),
            pltpu.VMEM((2 * BINS, width), jnp.float32),
            pltpu.VMEM((GROUPS, 64, 128), jnp.float32),
            pltpu.VMEM((windows, GROUPS, 16, width), jnp.bfloat16),
            pltpu.VMEM((hosts, GROUPS // 2, SLOTS, 128), jnp.bfloat16),
            dma((windows, 8)),
            dma,
            dma((windows, blocks)),
            dma((windows, blocks)),
            dma((3, windows)),
            dma((3, windows)),
            dma((4,)),
            dma((4,)),
            dma((windows,)),
            dma((3, 4)),
            dma((3, 4)),
        ],
        compiler_params=pltpu.CompilerParams(collective_id=0, has_side_effects=True, vmem_limit_bytes=48 << 20),
    )(record, tables, basis, offsets, sources)


def correlate(white_ref, rows_ref, lag_ref, out_ref, cross):
    hosts, windows = white_ref.shape[:2]
    used = cross.shape[0]

    @pl.when(pl.program_id(0) == 0)
    def _():
        lane = lax.broadcasted_iota(jnp.int32, (SLOTS, 128), 1)
        left = lane < 64
        real = lane % 16 < 8
        own = lax.broadcasted_iota(jnp.int32, (8, 256), 1) % 8 == lax.broadcasted_iota(jnp.int32, (8, 256), 0)
        own = jnp.where(own, 1.0, 0.0).astype(jnp.float32)
        blank = jnp.zeros((16, white_ref.shape[4]), jnp.bfloat16)

        def pair(at, _):
            tiles = [rows_ref[j, at].astype(jnp.float32) for j in range(hosts)]
            for odd in range(2):
                halves, turned = [], []
                for j in range(0, hosts, 2):
                    if odd:
                        both = jnp.where(left, pltpu.roll(tiles[j], 64, 1), tiles[j + 1])
                    else:
                        both = jnp.where(left, tiles[j], pltpu.roll(tiles[j + 1], 64, 1))
                    halves.append(both)
                    turned.append(jnp.where(real, pltpu.roll(both, 120, 1), -pltpu.roll(both, 8, 1)))
                first = jnp.concatenate(halves, axis=1)[:used]
                second = jnp.concatenate(turned, axis=1)[:used]
                spread = jnp.stack([first[:, None, :] * own[None], second[:, None, :] * own[None]], axis=1)
                spread = spread.reshape(used * 16, 256).astype(jnp.bfloat16)
                group = at * 2 + odd
                parts = []
                for j in range(hosts):
                    parts += [white_ref[j, w, group] for w in range(windows)] + [blank]
                found = jnp.dot(spread, jnp.concatenate(parts, axis=0), preferred_element_type=jnp.float32)
                cross[:, group] = found.astype(jnp.bfloat16).reshape(used, 16, -1)
            return 0

        lax.fori_loop(0, GROUPS // 2, pair, 0, unroll=4)

    spectrum = cross[pl.program_id(0)].reshape(2 * BINS, -1)
    found = jnp.dot(lag_ref[...], spectrum, preferred_element_type=jnp.float32)
    out_ref[0] = (found[:LAGS] + found[LAGS:]).astype(jnp.bfloat16)


def correlations(white, rows, total, used):
    hosts, windows, _, _, width = white.shape
    lags = jnp.asarray(np.concatenate(split_pair(lag_matrix(1 / math.sqrt(total * BINS)))))
    return pl.pallas_call(
        correlate,
        grid=(used,),
        out_shape=jax.ShapeDtypeStruct((used, LAGS, width), jnp.bfloat16),
        in_specs=[
            pl.BlockSpec(white.shape, lambda s: (0,) * 5),
            pl.BlockSpec(rows.shape, lambda s: (0,) * 4),
            pl.BlockSpec((2 * LAGS, 2 * BINS), lambda s: (0, 0)),
        ],
        out_specs=pl.BlockSpec((1, LAGS, width), lambda s: (s, 0, 0)),
        scratch_shapes=[pltpu.VMEM((used, GROUPS, 16, width), jnp.bfloat16)],
        compiler_params=pltpu.CompilerParams(vmem_limit_bytes=32 << 20),
    )(white, rows, lags)


def body(record, offsets, sources):
    windows, count, channels = record.shape
    blocks, hosts = lax.axis_size("chan"), lax.axis_size("win")
    width = channels // blocks
    per = sources.shape[1] // hosts
    basis = jnp.asarray(np.concatenate(split_pair(sample_basis(count).T)))
    tables = jnp.asarray(spectrum_tables(count, blocks))
    white, rows = exchanged(record, tables, basis, offsets, sources, blocks, hosts)
    out = correlations(white, rows, windows * hosts, ROUNDS * per)
    return out.reshape(ROUNDS, per, LAGS, width)


def solution(mesh):
    return jax.shard_map(
        body,
        mesh=mesh,
        in_specs=(P("win", "chan", None), P("win"), P()),
        out_specs=P(None, "win", None, "chan"),
        check_vma=False,
    )
```

```python
import math

import jax
import jax.numpy as jnp
import numpy as np
from jax import lax
from jax.experimental import pallas as pl
from jax.experimental.pallas import tpu as pltpu
from jax.sharding import PartitionSpec as P

SAMPLES = 7680
BINS = 256
F0 = 16
LAGS = 256
LAG_STEP = 8
ROUNDS = 3
RANK = 32
GROUPS = BINS // 8
SLOTS = 16
PIECES = 4
EARLY = 2
MESH = pl.DeviceIdType.MESH


def sample_basis(count):
    half = (F0 + BINS) / SAMPLES
    at = np.arange(count)
    matrix = np.diag(((count - 1) / 2 - at) ** 2 * math.cos(2 * math.pi * half))
    side = at[1:] * (count - at[1:]) / 2
    matrix = matrix + np.diag(side, 1) + np.diag(side, -1)
    vectors = np.linalg.eigh(matrix)[1][:, ::-1][:, :RANK]
    return vectors * np.where(vectors[0] < 0, -1.0, 1.0)


def spectrum_tables(count, blocks):
    basis = sample_basis(count)
    middle = (count - 1) / 2
    at = np.arange(count) - middle
    terms = []
    for step, weight in ((0, 0.5), (1, -0.25), (-1, -0.25)):
        freqs = np.arange(BINS) + F0 + step
        wave = np.exp(-2j * math.pi / SAMPLES * np.outer(freqs, at)) @ basis
        turn = np.exp(-2j * math.pi / SAMPLES * np.outer(freqs, count * np.arange(blocks) + middle))
        table = weight * (turn[:, :, None] * wave[:, None, :]).reshape(BINS, blocks, 2, RANK // 2)
        terms.append(table.transpose(0, 2, 1, 3).reshape(BINS, blocks * RANK))
    own, above, below = terms
    return np.stack([p for t in (own, above + below, above - below) for p in (t.real, t.imag)]).astype(np.float32)


def lag_matrix(scale):
    shifts = LAG_STEP * (np.arange(LAGS) - LAGS // 2)
    phase = shifts[:, None] * (np.arange(BINS) + F0)[None, :] % SAMPLES
    angle = 2 * math.pi / SAMPLES * phase
    both = np.stack([np.cos(angle), np.sin(angle)], axis=1).reshape(LAGS, 2, GROUPS, 8)
    return (both.transpose(0, 2, 1, 3).reshape(LAGS, 2 * BINS) * scale).astype(np.float32)


def split_pair(array):
    high = array.astype(jnp.bfloat16)
    return high, (array - high.astype(array.dtype)).astype(jnp.bfloat16)


def exchange(
    record, tables, basis_in, lags_in, offsets_in, sources_in, out,
    held, parts, basis, lags, offsets, sources, masked, turns, message, arrived, coded, picked, full, spectra, columns,
    white, rows, rows_in, spread, cross, partial, done,
    load_sem, const_sem, send_sem, recv_sem, pass_sem, take_sem, rows_send, rows_recv, pick_send, pick_recv, out_sem,
):
    windows, chunks = held.shape[:2]
    blocks = message.shape[1]
    samples = held.shape[2]
    slots = sources.shape[1] // 4
    me, win = lax.axis_index("chan"), lax.axis_index("win")

    def load(w, k):
        at = (me // 4) ^ k
        source = record.at[w, :, pl.ds(pl.multiple_of(at * 1024, 1024), 1024)]
        return pltpu.make_async_copy(source, held.at[w, k], load_sem.at[w, k])

    def start_load(i, _):
        load(i // chunks, i % chunks).start()
        return 0

    lax.fori_loop(0, chunks, start_load, 0)
    pairs = ((offsets_in, offsets), (sources_in, sources), (basis_in, basis), (tables, parts), (lags_in, lags))
    consts = [pltpu.make_async_copy(a, b, const_sem.at[i]) for i, (a, b) in enumerate(pairs)]
    for copy in consts[:3]:
        copy.start()
    lax.fori_loop(chunks, windows * chunks, start_load, 0)
    for copy in consts[3:]:
        copy.start()

    barrier = pltpu.get_barrier_semaphore()

    def greet(k, _):
        pl.semaphore_signal(barrier, inc=1, device_id=(win, me ^ k), device_id_type=MESH)
        return 0

    lax.fori_loop(1, blocks, greet, 0)
    for k in (1, 2, 3):
        pl.semaphore_signal(barrier, inc=1, device_id=(win ^ k, me), device_id_type=MESH)

    for copy in consts[:3]:
        copy.wait()

    for w in range(windows):
        time = lax.broadcasted_iota(jnp.int32, basis.shape, 1) + (me * samples - offsets[w])
        inside = (time >= 0) & (time < SAMPLES)
        masked[w] = jnp.where(inside, basis[...].astype(jnp.float32), 0.0).astype(jnp.bfloat16)

    wide = lax.broadcasted_iota(jnp.int32, turns.shape, 1)
    freq = jnp.where(wide % 4 < 2, lax.broadcasted_iota(jnp.int32, turns.shape, 0) + F0, 1)
    shift = jnp.zeros(turns.shape, jnp.int32)
    for w in range(windows):
        shift = jnp.where(wide // 4 == w, offsets[w], shift)
    turn = (freq * shift).astype(jnp.float32)
    turn = turn - SAMPLES * jnp.floor(turn * (1 / SAMPLES))
    turn = turn * (2 * math.pi / SAMPLES) - jnp.where(wide % 2 == 1, math.pi / 2, 0.0)
    turns[...] = jnp.cos(turn)

    lane = lax.broadcasted_iota(jnp.int32, (16, 128), 1)
    columns[:, 48:, :] = jnp.zeros((GROUPS, 16, 128), jnp.float32)

    def project(w):
        def chunk(k, _):
            load(w, k).wait()
            at = (me // 4) ^ k
            found = jnp.dot(masked[w], held[w, k], preferred_element_type=jnp.float32)
            found = (found[:RANK] + found[RANK:]).astype(jnp.bfloat16)
            for i in range(4):
                part = found[:, 256 * i : 256 * (i + 1)]
                message[w, at * 4 + i, :, 0:256] = part[:16]
                message[w, at * 4 + i, :, 256:512] = part[16:]
            for i in range(8):
                coded[w, at * 8 + i] = found[:, 128 * i : 128 * (i + 1)]
            return 0

        lax.fori_loop(0, chunks, chunk, 0)

        arrived[w, me] = message[w, me]

    def choose(w, _):
        wide = lax.broadcasted_iota(jnp.int32, (RANK, 128), 1)

        def pick(i, total):
            slot = i // 12 * SLOTS + i % 12
            source = sources[i % 12 // slots, i // 12 * slots + i % slots]
            tile = coded[w, source // 128].astype(jnp.float32)
            value = jnp.sum(jnp.where(wide == source % 128, tile, 0.0), axis=1, keepdims=True)
            total = jnp.where(lane == slot, value[:16], total)
            return jnp.where(lane == slot + 64, value[16:], total)

        chosen = lax.fori_loop(0, ROUNDS * slots * 4, pick, jnp.zeros((16, 128), jnp.float32), unroll=8)
        picked[me // 8, me // 4 % 2, me % 4, w] = chosen.astype(jnp.bfloat16)
        return 0

    def cast(step, k):
        x, z, y = me // 8, me // 4 % 2, me % 4
        part = (picked.at[x, z, y], picked.at[x, :, y], picked.at[:, :, y])[step]
        return pltpu.make_async_remote_copy(
            part, part, pick_send.at[step, k], pick_recv.at[step, k],
            device_id=(win, me ^ (4, 8 * k, k)[step]), device_id_type=MESH,
        )

    def caught(step, k):
        there = me ^ (4, 8 * k, k)[step]
        x, z, y = there // 8, there // 4 % 2, there % 4
        part = (picked.at[x, z, y], picked.at[x, :, y], picked.at[:, :, y])[step]
        return pltpu.make_async_remote_copy(
            part, part, pick_send.at[step, k], pick_recv.at[step, k],
            device_id=(win, there), device_id_type=MESH,
        )

    def send(w, k):
        return pltpu.make_async_remote_copy(
            message.at[w, me ^ k], arrived.at[w, me], send_sem.at[w, k], recv_sem.at[w, me],
            device_id=(win, me ^ k), device_id_type=MESH,
        )

    def receive(w, k):
        return pltpu.make_async_remote_copy(
            message.at[w, me ^ k], arrived.at[w, me ^ k], send_sem.at[w, k], recv_sem.at[w, me ^ k],
            device_id=(win, me ^ k), device_id_type=MESH,
        )

    def start_sends(w):
        def one(k, _):
            send(w, k).start()
            return 0

        lax.fori_loop(1, blocks, one, 0, unroll=8)

    project(0)
    pl.semaphore_wait(barrier, blocks - 1 + 3)
    start_sends(0)
    project(1)
    start_sends(1)
    project(2)
    lax.fori_loop(0, windows, choose, 0)
    cast(0, 1).start()
    start_sends(2)

    consts[3].wait()

    def tabulate(w, g):
        own_re, own_im, sum_re, sum_im, dif_re, dif_im = [parts[t, pl.ds(pl.multiple_of(g * 8, 8), 8)] for t in range(6)]
        turn = turns[pl.ds(pl.multiple_of(g * 8, 8), 8), :][:, 4 * w : 4 * w + 4]
        c, s = turn[:, 2:3], turn[:, 3:4]
        re = own_re + c * sum_re - s * dif_im
        im = own_im + c * sum_im + s * dif_re
        c, s = turn[:, 0:1], turn[:, 1:2]
        both = jnp.concatenate([c * re - s * im, c * im + s * re], axis=0)
        high = both.astype(jnp.bfloat16)
        full[w, 0, g] = high
        full[w, 1, g] = (both - high.astype(jnp.float32)).astype(jnp.bfloat16)
        return 0

    for w in range(windows):
        lax.fori_loop(0, GROUPS, lambda g, _, w=w: tabulate(w, g), 0, unroll=4)

    piece = GROUPS // PIECES

    def hand(w, k, p):
        part = pl.ds(p * piece, piece)
        return pltpu.make_async_remote_copy(
            white.at[0, w, part], white.at[k, w, part], pass_sem.at[k - 1, w, p], take_sem.at[k - 1, w, p],
            device_id=(win ^ k, me), device_id_type=MESH,
        )

    def relay(w, p):
        part = pl.ds(p * piece, piece)
        return pltpu.make_async_remote_copy(
            white.at[2, w, part], white.at[3, w, part], pass_sem.at[2, w, p], take_sem.at[2, w, p],
            device_id=(win ^ 1, me), device_id_type=MESH,
        )

    def whiten(w):
        def wait_one(k, _):
            receive(w, k).wait_recv()
            return 0

        lax.fori_loop(1, blocks, wait_one, 0, unroll=8)
        first = arrived[w, :, :, 0:256].reshape(blocks * 16, 256)
        second = arrived[w, :, :, 256:512].reshape(blocks * 16, 256)
        cut = blocks * 16

        def tile(m, power):
            found = jnp.zeros((128, 256), jnp.float32)
            for half in range(2):
                table = full[w, half, pl.ds(m * 8, 8)].reshape(128, 2 * cut)
                found += jnp.dot(table[:, :cut], first, preferred_element_type=jnp.float32)
                found += jnp.dot(table[:, cut:], second, preferred_element_type=jnp.float32)
            spectra[pl.ds(pl.multiple_of(m * 128, 128), 128)] = found
            return power + jnp.sum(found * found, axis=0, keepdims=True)

        power = lax.fori_loop(0, 4, tile, jnp.zeros((1, 256), jnp.float32))
        scale = lax.rsqrt(power * (1 / (2 * BINS)) + 1e-06)

        def norm(m, _):
            found = (spectra[pl.ds(pl.multiple_of(m * 128, 128), 128)] * scale).astype(jnp.bfloat16)
            white[0, w, pl.ds(m * 8, 8)] = found.reshape(8, 16, 256)
            return 0

        lax.fori_loop(0, 4, norm, 0, unroll=2)
        for p in range(PIECES if w < windows - 1 else EARLY):
            hand(w, 2, p).start()
            hand(w, 1, p).start()

    def whiten_picked(w, _):
        extra = picked[:, :, :, w].reshape(blocks * 16, 128)
        cut = blocks * 16

        def tile(m, power):
            low = jnp.zeros((128, 128), jnp.float32)
            top = jnp.zeros((128, 128), jnp.float32)
            for half in range(1):
                table = full[w, half, pl.ds(m * 8, 8)].reshape(128, 2 * cut)
                low += jnp.dot(table[:, :cut], extra, preferred_element_type=jnp.float32)
                top += jnp.dot(table[:, cut:], extra, preferred_element_type=jnp.float32)
            found = low + pltpu.roll(top, 64, 1)
            spectra[pl.ds(pl.multiple_of(m * 128, 128), 128), 0:128] = found
            return power + jnp.sum(found * found, axis=0, keepdims=True)

        power = lax.fori_loop(0, 4, tile, jnp.zeros((1, 128), jnp.float32))
        scale = lax.rsqrt(power * (1 / (2 * BINS)) + 1e-06)

        def norm(m, _):
            found = spectra[pl.ds(pl.multiple_of(m * 128, 128), 128), 0:128] * scale
            columns[pl.ds(m * 8, 8), pl.ds(pl.multiple_of(w * 16, 16), 16)] = (
                found.astype(jnp.bfloat16).astype(jnp.float32).reshape(8, 16, 128)
            )
            return 0

        lax.fori_loop(0, 4, norm, 0, unroll=2)
        return 0

    caught(0, 1).wait_recv()
    for k in (2, 1, 3):
        cast(1, k).start()
    whiten(0)
    for k in (1, 2, 3):
        caught(1, k).wait_recv()
    for k in (2, 1, 3):
        cast(2, k).start()
    whiten(1)
    whiten(2)
    for k in (1, 2, 3):
        caught(2, k).wait_recv()
    lax.fori_loop(0, windows, whiten_picked, 0)

    def turn_over(at, _):
        block = columns[pl.ds(at * 2, 2)].reshape(128, 128).T
        rows[:, at] = block[:64].reshape(4, SLOTS, 128).astype(jnp.bfloat16)
        return 0

    lax.fori_loop(0, GROUPS // 2, turn_over, 0, unroll=4)

    def deal(k):
        return pltpu.make_async_remote_copy(
            rows.at[win ^ k], rows_in.at[k], rows_send.at[k], rows_recv.at[k],
            device_id=(win ^ k, me), device_id_type=MESH,
        )

    for k in (2, 3, 1):
        deal(k).start()
    for p in range(EARLY, PIECES):
        hand(windows - 1, 2, p).start()
        hand(windows - 1, 1, p).start()
    rows_in[0] = rows[win]

    def forward(i, _):
        hand(i // PIECES, 2, i % PIECES).wait_recv()
        relay(i // PIECES, i % PIECES).start()
        return 0

    lax.fori_loop(0, (windows - 1) * PIECES, forward, 0)
    lane = lax.broadcasted_iota(jnp.int32, (SLOTS, 128), 1)
    left = lane < 64
    real = lane % 16 < 8
    own = lax.broadcasted_iota(jnp.int32, (8, 128), 1) % 8 == lax.broadcasted_iota(jnp.int32, (8, 128), 0)
    own = jnp.where(own, 1.0, 0.0).astype(jnp.float32)
    used = done.shape[0]

    def build(at, half):
        tiles = [rows_in[2 * half + j, at].astype(jnp.float32) for j in range(2)]
        for odd in range(2):
            if odd:
                both = jnp.where(left, pltpu.roll(tiles[0], 64, 1), tiles[1])
            else:
                both = jnp.where(left, tiles[0], pltpu.roll(tiles[1], 64, 1))
            turned = jnp.where(real, pltpu.roll(both, 120, 1), -pltpu.roll(both, 8, 1))
            table = jnp.stack([both[:used, None, :] * own[None], turned[:used, None, :] * own[None]], axis=1)
            spread[at * 2 + odd, :, 128 * half : 128 * (half + 1)] = table.reshape(used * 16, 128).astype(jnp.bfloat16)

    def build_half(half):
        def one(at, _):
            build(at, half)
            return 0

        lax.fori_loop(0, GROUPS // 2, one, 0, unroll=4)

    def arrive(i, _):
        hand(i // PIECES, 1, i % PIECES).wait_recv()
        relay(i // PIECES, i % PIECES).wait_recv()
        return 0

    blank = jnp.zeros((16, white.shape[4]), jnp.bfloat16)

    def multiply(g, _):
        pieces = []
        for j in range(4):
            pieces += [white[j, w, g] for w in range(windows)] + [blank]
        found = jnp.dot(spread[g], jnp.concatenate(pieces, axis=0), preferred_element_type=jnp.float32)
        cross[:, g] = found.astype(jnp.bfloat16).reshape(used, 16, -1)
        return 0

    def lagged(s, half):
        part = cross[s, GROUPS // 2 * half : GROUPS // 2 * (half + 1)].reshape(BINS, -1)
        return jnp.dot(lags[:, BINS * half : BINS * (half + 1)], part, preferred_element_type=jnp.float32)

    def leave(s):
        return pltpu.make_async_copy(done.at[s], out.at[s], out_sem.at[s])

    def first_half(s, _):
        partial[s] = lagged(s, 0)
        return 0

    def second_half(s, _):
        done[s] = (partial[s] + lagged(s, 1)).astype(jnp.bfloat16)
        leave(s).start()
        return 0

    last = (windows - 1) * PIECES
    deal(1).wait_recv()
    build_half(0)
    consts[4].wait()
    lax.fori_loop(0, last, arrive, 0)
    forward(last, 0)
    for k in (2, 3):
        deal(k).wait_recv()
    build_half(1)
    for p in range(PIECES):
        if p + 1 < PIECES:
            forward(last + p + 1, 0)
        arrive(last + p, 0)
        lax.fori_loop(p * piece, (p + 1) * piece, multiply, 0, unroll=4)
        if p == PIECES // 2 - 1:
            lax.fori_loop(0, used, first_half, 0, unroll=2)
    lax.fori_loop(0, used, second_half, 0, unroll=2)

    def finish(i, _):
        w, p = i // PIECES, i % PIECES
        hand(w, 1, p).wait_send()
        hand(w, 2, p).wait_send()
        relay(w, p).wait_send()
        return 0

    def sent(w, _):
        def one(k, _):
            send(w, k).wait_send()
            return 0

        lax.fori_loop(1, blocks, one, 0, unroll=8)
        return 0

    lax.fori_loop(0, windows * PIECES, finish, 0)
    lax.fori_loop(0, windows, sent, 0)
    cast(0, 1).wait_send()
    for k in (1, 2, 3):
        cast(1, k).wait_send()
        cast(2, k).wait_send()
        deal(k).wait_send()

    def left_all(s, _):
        leave(s).wait()
        return 0

    lax.fori_loop(0, used, left_all, 0)


def body(record, offsets, sources):
    windows, count, channels = record.shape
    blocks, hosts = lax.axis_size("chan"), lax.axis_size("win")
    width = channels // blocks
    per = sources.shape[1] // hosts
    used = ROUNDS * per
    basis = jnp.asarray(np.concatenate(split_pair(sample_basis(count).T)))
    tables = jnp.asarray(spectrum_tables(count, blocks))
    scale = 1 / math.sqrt(windows * hosts * BINS)
    lags = jnp.asarray(lag_matrix(scale).astype(jnp.bfloat16))
    dma = pltpu.SemaphoreType.DMA
    anywhere = pl.BlockSpec(memory_space=pl.ANY)
    out = pl.pallas_call(
        exchange,
        out_shape=jax.ShapeDtypeStruct((used, LAGS, width), jnp.bfloat16),
        in_specs=[anywhere] * 6,
        out_specs=anywhere,
        scratch_shapes=[
            pltpu.VMEM((windows, 8, count, channels // 8), jnp.bfloat16),
            pltpu.VMEM(tables.shape, jnp.float32),
            pltpu.VMEM(basis.shape, jnp.bfloat16),
            pltpu.VMEM(lags.shape, jnp.bfloat16),
            pltpu.SMEM(offsets.shape, jnp.int32),
            pltpu.SMEM(sources.shape, jnp.int32),
            pltpu.VMEM((windows,) + basis.shape, jnp.bfloat16),
            pltpu.VMEM((BINS, 128), jnp.float32),
            pltpu.VMEM((windows, blocks, 16, 2 * width), jnp.bfloat16),
            pltpu.VMEM((windows, blocks, 16, 2 * width), jnp.bfloat16),
            pltpu.VMEM((windows, channels // 128, RANK, 128), jnp.bfloat16),
            pltpu.VMEM((4, 2, 4, windows, 16, 128), jnp.bfloat16),
            pltpu.VMEM((windows, 2, GROUPS, 16, blocks * RANK), jnp.bfloat16),
            pltpu.VMEM((2 * BINS, width), jnp.float32),
            pltpu.VMEM((GROUPS, 64, 128), jnp.float32),
            pltpu.VMEM((hosts, windows, GROUPS, 16, width), jnp.bfloat16),
            pltpu.VMEM((hosts, GROUPS // 2, SLOTS, 128), jnp.bfloat16),
            pltpu.VMEM((hosts, GROUPS // 2, SLOTS, 128), jnp.bfloat16),
            pltpu.VMEM((GROUPS, used * 16, 256), jnp.bfloat16),
            pltpu.VMEM((used, GROUPS, 16, width), jnp.bfloat16),
            pltpu.VMEM((used, LAGS, width), jnp.float32),
            pltpu.VMEM((used, LAGS, width), jnp.bfloat16),
            dma((windows, 8)),
            dma((5,)),
            dma((windows, blocks)),
            dma((windows, blocks)),
            dma((3, windows, PIECES)),
            dma((3, windows, PIECES)),
            dma((4,)),
            dma((4,)),
            dma((3, 4)),
            dma((3, 4)),
            dma((used,)),
        ],
        compiler_params=pltpu.CompilerParams(collective_id=0, has_side_effects=True, vmem_limit_bytes=56 << 20),
    )(record, tables, basis, lags, offsets, sources)
    return out.reshape(ROUNDS, per, LAGS, width)


def solution(mesh):
    return jax.shard_map(
        body,
        mesh=mesh,
        in_specs=(P("win", "chan", None), P("win"), P()),
        out_specs=P(None, "win", None, "chan"),
        check_vma=False,
    )
```

```python
import math

import jax
import jax.numpy as jnp
import numpy as np
from jax import lax
from jax.experimental import pallas as pl
from jax.experimental.pallas import tpu as pltpu
from jax.sharding import PartitionSpec as P

SAMPLES = 7680
BINS = 256
F0 = 16
LAGS = 256
LAG_STEP = 8
ROUNDS = 3
RANK = 32
GROUPS = BINS // 8
SLOTS = 16
PIECES = 4
EARLY = 1
MESH = pl.DeviceIdType.MESH


def sample_basis(count):
    half = (F0 + BINS) / SAMPLES
    at = np.arange(count)
    matrix = np.diag(((count - 1) / 2 - at) ** 2 * math.cos(2 * math.pi * half))
    side = at[1:] * (count - at[1:]) / 2
    matrix = matrix + np.diag(side, 1) + np.diag(side, -1)
    vectors = np.linalg.eigh(matrix)[1][:, ::-1][:, :RANK]
    return vectors * np.where(vectors[0] < 0, -1.0, 1.0)


def spectrum_tables(count, blocks):
    basis = sample_basis(count)
    middle = (count - 1) / 2
    at = np.arange(count) - middle
    terms = []
    for step, weight in ((0, 0.5), (1, -0.25), (-1, -0.25)):
        freqs = np.arange(BINS) + F0 + step
        wave = np.exp(-2j * math.pi / SAMPLES * np.outer(freqs, at)) @ basis
        turn = np.exp(-2j * math.pi / SAMPLES * np.outer(freqs, count * np.arange(blocks) + middle))
        table = weight * (turn[:, :, None] * wave[:, None, :]).reshape(BINS, blocks, 2, RANK // 2)
        terms.append(table.transpose(0, 2, 1, 3).reshape(BINS, blocks * RANK))
    own, above, below = terms
    return np.stack([p for t in (own, above + below, above - below) for p in (t.real, t.imag)]).astype(np.float32)


def lag_matrix(scale):
    shifts = LAG_STEP * (np.arange(LAGS) - LAGS // 2)
    phase = shifts[:, None] * (np.arange(BINS) + F0)[None, :] % SAMPLES
    angle = 2 * math.pi / SAMPLES * phase
    both = np.stack([np.cos(angle), np.sin(angle)], axis=1).reshape(LAGS, 2, GROUPS, 8)
    return (both.transpose(0, 2, 1, 3).reshape(LAGS, 2 * BINS) * scale).astype(np.float32)


def split_pair(array):
    high = array.astype(jnp.bfloat16)
    return high, (array - high.astype(array.dtype)).astype(jnp.bfloat16)


def exchange(
    record, tables, basis_in, lags_in, offsets_in, sources_in, out,
    held, parts, basis, lags, offsets, sources, masked, turns, message, arrived, coded, picked, full, spectra, columns,
    white, rows, rows_in, spread, cross, partial, done,
    load_sem, const_sem, send_sem, recv_sem, pass_sem, take_sem, rows_send, rows_recv, pick_send, pick_recv, out_sem,
):
    windows, chunks = held.shape[:2]
    blocks = message.shape[1]
    samples = held.shape[2]
    slots = sources.shape[1] // 4
    me, win = lax.axis_index("chan"), lax.axis_index("win")

    def load(w, k):
        at = (me // 4) ^ k
        source = record.at[w, :, pl.ds(pl.multiple_of(at * 1024, 1024), 1024)]
        return pltpu.make_async_copy(source, held.at[w, k], load_sem.at[w, k])

    def start_load(i, _):
        load(i // chunks, i % chunks).start()
        return 0

    lax.fori_loop(0, chunks, start_load, 0)
    pairs = ((offsets_in, offsets), (sources_in, sources), (basis_in, basis), (tables, parts), (lags_in, lags))
    consts = [pltpu.make_async_copy(a, b, const_sem.at[i]) for i, (a, b) in enumerate(pairs)]
    for copy in consts[:3]:
        copy.start()
    lax.fori_loop(chunks, windows * chunks, start_load, 0)
    for copy in consts[3:]:
        copy.start()

    barrier = pltpu.get_barrier_semaphore()

    def greet(k, _):
        pl.semaphore_signal(barrier, inc=1, device_id=(win, me ^ k), device_id_type=MESH)
        return 0

    lax.fori_loop(1, blocks, greet, 0)
    for k in (1, 2, 3):
        pl.semaphore_signal(barrier, inc=1, device_id=(win ^ k, me), device_id_type=MESH)

    for copy in consts[:3]:
        copy.wait()

    for w in range(windows):
        time = lax.broadcasted_iota(jnp.int32, basis.shape, 1) + (me * samples - offsets[w])
        inside = (time >= 0) & (time < SAMPLES)
        masked[w] = jnp.where(inside, basis[...].astype(jnp.float32), 0.0).astype(jnp.bfloat16)

    wide = lax.broadcasted_iota(jnp.int32, turns.shape, 1)
    freq = jnp.where(wide % 4 < 2, lax.broadcasted_iota(jnp.int32, turns.shape, 0) + F0, 1)
    shift = jnp.zeros(turns.shape, jnp.int32)
    for w in range(windows):
        shift = jnp.where(wide // 4 == w, offsets[w], shift)
    turn = (freq * shift).astype(jnp.float32)
    turn = turn - SAMPLES * jnp.floor(turn * (1 / SAMPLES))
    turn = turn * (2 * math.pi / SAMPLES) - jnp.where(wide % 2 == 1, math.pi / 2, 0.0)
    turns[...] = jnp.cos(turn)

    lane = lax.broadcasted_iota(jnp.int32, (16, 128), 1)
    columns[:, 48:, :] = jnp.zeros((GROUPS, 16, 128), jnp.float32)

    def project(w):
        def chunk(k, _):
            load(w, k).wait()
            at = (me // 4) ^ k
            found = jnp.dot(masked[w], held[w, k], preferred_element_type=jnp.float32)
            found = (found[:RANK] + found[RANK:]).astype(jnp.bfloat16)
            for i in range(4):
                part = found[:, 256 * i : 256 * (i + 1)]
                message[w, at * 4 + i, :, 0:256] = part[:16]
                message[w, at * 4 + i, :, 256:512] = part[16:]
            for i in range(8):
                coded[w, at * 8 + i] = found[:, 128 * i : 128 * (i + 1)]
            return 0

        lax.fori_loop(0, chunks, chunk, 0)

        arrived[w, me] = message[w, me]

    def choose(w, _):
        wide = lax.broadcasted_iota(jnp.int32, (RANK, 128), 1)

        def pick(i, total):
            slot = i // 12 * SLOTS + i % 12
            source = sources[i % 12 // slots, i // 12 * slots + i % slots]
            tile = coded[w, source // 128].astype(jnp.float32)
            value = jnp.sum(jnp.where(wide == source % 128, tile, 0.0), axis=1, keepdims=True)
            total = jnp.where(lane == slot, value[:16], total)
            return jnp.where(lane == slot + 64, value[16:], total)

        chosen = lax.fori_loop(0, ROUNDS * slots * 4, pick, jnp.zeros((16, 128), jnp.float32), unroll=8)
        picked[me // 8, me // 4 % 2, me % 4, w] = chosen.astype(jnp.bfloat16)
        return 0

    def cast(step, k):
        x, z, y = me // 8, me // 4 % 2, me % 4
        part = (picked.at[x, z, y], picked.at[x, :, y], picked.at[:, :, y])[step]
        return pltpu.make_async_remote_copy(
            part, part, pick_send.at[step, k], pick_recv.at[step, k],
            device_id=(win, me ^ (4, 8 * k, k)[step]), device_id_type=MESH,
        )

    def caught(step, k):
        there = me ^ (4, 8 * k, k)[step]
        x, z, y = there // 8, there // 4 % 2, there % 4
        part = (picked.at[x, z, y], picked.at[x, :, y], picked.at[:, :, y])[step]
        return pltpu.make_async_remote_copy(
            part, part, pick_send.at[step, k], pick_recv.at[step, k],
            device_id=(win, there), device_id_type=MESH,
        )

    def send(w, k):
        return pltpu.make_async_remote_copy(
            message.at[w, me ^ k], arrived.at[w, me], send_sem.at[w, k], recv_sem.at[w, me],
            device_id=(win, me ^ k), device_id_type=MESH,
        )

    def receive(w, k):
        return pltpu.make_async_remote_copy(
            message.at[w, me ^ k], arrived.at[w, me ^ k], send_sem.at[w, k], recv_sem.at[w, me ^ k],
            device_id=(win, me ^ k), device_id_type=MESH,
        )

    def start_sends(w):
        def one(k, _):
            send(w, k).start()
            return 0

        lax.fori_loop(1, blocks, one, 0, unroll=8)

    project(0)
    pl.semaphore_wait(barrier, blocks - 1 + 3)
    start_sends(0)
    project(1)
    start_sends(1)
    project(2)
    start_sends(2)
    lax.fori_loop(0, windows, choose, 0)
    cast(0, 1).start()

    consts[3].wait()

    def tabulate(w, g):
        own_re, own_im, sum_re, sum_im, dif_re, dif_im = [parts[t, pl.ds(pl.multiple_of(g * 8, 8), 8)] for t in range(6)]
        turn = turns[pl.ds(pl.multiple_of(g * 8, 8), 8), :][:, 4 * w : 4 * w + 4]
        c, s = turn[:, 2:3], turn[:, 3:4]
        re = own_re + c * sum_re - s * dif_im
        im = own_im + c * sum_im + s * dif_re
        c, s = turn[:, 0:1], turn[:, 1:2]
        both = jnp.concatenate([c * re - s * im, c * im + s * re], axis=0)
        high = both.astype(jnp.bfloat16)
        full[w, 0, g] = high
        full[w, 1, g] = (both - high.astype(jnp.float32)).astype(jnp.bfloat16)
        return 0

    for w in range(windows):
        lax.fori_loop(0, GROUPS, lambda g, _, w=w: tabulate(w, g), 0, unroll=4)

    piece = GROUPS // PIECES

    def hand(w, k, p):
        part = pl.ds(p * piece, piece)
        return pltpu.make_async_remote_copy(
            white.at[0, w, part], white.at[k, w, part], pass_sem.at[k - 1, w, p], take_sem.at[k - 1, w, p],
            device_id=(win ^ k, me), device_id_type=MESH,
        )

    def relay(w, p):
        part = pl.ds(p * piece, piece)
        return pltpu.make_async_remote_copy(
            white.at[2, w, part], white.at[3, w, part], pass_sem.at[2, w, p], take_sem.at[2, w, p],
            device_id=(win ^ 1, me), device_id_type=MESH,
        )

    def whiten(w):
        def wait_one(k, _):
            receive(w, k).wait_recv()
            return 0

        lax.fori_loop(1, blocks, wait_one, 0, unroll=8)
        first = arrived[w, :, :, 0:256].reshape(blocks * 16, 256)
        second = arrived[w, :, :, 256:512].reshape(blocks * 16, 256)
        cut = blocks * 16

        def tile(m, power):
            found = jnp.zeros((128, 256), jnp.float32)
            for half in range(2):
                table = full[w, half, pl.ds(m * 8, 8)].reshape(128, 2 * cut)
                found += jnp.dot(table[:, :cut], first, preferred_element_type=jnp.float32)
                found += jnp.dot(table[:, cut:], second, preferred_element_type=jnp.float32)
            spectra[pl.ds(pl.multiple_of(m * 128, 128), 128)] = found
            return power + jnp.sum(found * found, axis=0, keepdims=True)

        power = lax.fori_loop(0, 4, tile, jnp.zeros((1, 256), jnp.float32))
        scale = lax.rsqrt(power * (1 / (2 * BINS)) + 1e-06)

        def norm(m, _):
            found = (spectra[pl.ds(pl.multiple_of(m * 128, 128), 128)] * scale).astype(jnp.bfloat16)
            white[0, w, pl.ds(m * 8, 8)] = found.reshape(8, 16, 256)
            return 0

        lax.fori_loop(0, 4, norm, 0, unroll=2)
        for p in range(PIECES if w < windows - 1 else EARLY):
            hand(w, 2, p).start()
            hand(w, 1, p).start()

    def whiten_picked(w, _):
        extra = picked[:, :, :, w].reshape(blocks * 16, 128)
        cut = blocks * 16

        def tile(m, power):
            low = jnp.zeros((128, 128), jnp.float32)
            top = jnp.zeros((128, 128), jnp.float32)
            for half in range(1):
                table = full[w, half, pl.ds(m * 8, 8)].reshape(128, 2 * cut)
                low += jnp.dot(table[:, :cut], extra, preferred_element_type=jnp.float32)
                top += jnp.dot(table[:, cut:], extra, preferred_element_type=jnp.float32)
            found = low + pltpu.roll(top, 64, 1)
            spectra[pl.ds(pl.multiple_of(m * 128, 128), 128), 0:128] = found
            return power + jnp.sum(found * found, axis=0, keepdims=True)

        power = lax.fori_loop(0, 4, tile, jnp.zeros((1, 128), jnp.float32))
        scale = lax.rsqrt(power * (1 / (2 * BINS)) + 1e-06)

        def norm(m, _):
            found = spectra[pl.ds(pl.multiple_of(m * 128, 128), 128), 0:128] * scale
            columns[pl.ds(m * 8, 8), pl.ds(pl.multiple_of(w * 16, 16), 16)] = (
                found.astype(jnp.bfloat16).astype(jnp.float32).reshape(8, 16, 128)
            )
            return 0

        lax.fori_loop(0, 4, norm, 0, unroll=2)
        return 0

    caught(0, 1).wait_recv()
    for k in (2, 1, 3):
        cast(1, k).start()
    whiten(0)
    for k in (1, 2, 3):
        caught(1, k).wait_recv()
    for k in (2, 1, 3):
        cast(2, k).start()
    whiten(1)
    whiten(2)
    for k in (1, 2, 3):
        caught(2, k).wait_recv()
    lax.fori_loop(0, windows, whiten_picked, 0)

    def turn_over(at, _):
        block = columns[pl.ds(at * 2, 2)].reshape(128, 128).T
        rows[:, at] = block[:64].reshape(4, SLOTS, 128).astype(jnp.bfloat16)
        return 0

    lax.fori_loop(0, GROUPS // 2, turn_over, 0, unroll=4)

    def deal(k):
        return pltpu.make_async_remote_copy(
            rows.at[win ^ k], rows_in.at[k], rows_send.at[k], rows_recv.at[k],
            device_id=(win ^ k, me), device_id_type=MESH,
        )

    for k in (2, 3, 1):
        deal(k).start()
    for p in range(EARLY, PIECES):
        hand(windows - 1, 2, p).start()
        hand(windows - 1, 1, p).start()
    rows_in[0] = rows[win]

    def forward(i, _):
        hand(i // PIECES, 2, i % PIECES).wait_recv()
        relay(i // PIECES, i % PIECES).start()
        return 0

    lax.fori_loop(0, (windows - 1) * PIECES, forward, 0)
    lane = lax.broadcasted_iota(jnp.int32, (SLOTS, 128), 1)
    left = lane < 64
    real = lane % 16 < 8
    own = lax.broadcasted_iota(jnp.int32, (8, 128), 1) % 8 == lax.broadcasted_iota(jnp.int32, (8, 128), 0)
    own = jnp.where(own, 1.0, 0.0).astype(jnp.float32)
    used = done.shape[0]

    def build(at, half):
        tiles = [rows_in[2 * half + j, at].astype(jnp.float32) for j in range(2)]
        for odd in range(2):
            if odd:
                both = jnp.where(left, pltpu.roll(tiles[0], 64, 1), tiles[1])
            else:
                both = jnp.where(left, tiles[0], pltpu.roll(tiles[1], 64, 1))
            turned = jnp.where(real, pltpu.roll(both, 120, 1), -pltpu.roll(both, 8, 1))
            table = jnp.stack([both[:used, None, :] * own[None], turned[:used, None, :] * own[None]], axis=1)
            spread[at * 2 + odd, :, 128 * half : 128 * (half + 1)] = table.reshape(used * 16, 128).astype(jnp.bfloat16)

    def build_half(half):
        def one(at, _):
            build(at, half)
            return 0

        lax.fori_loop(0, GROUPS // 2, one, 0, unroll=4)

    def arrive(i, _):
        hand(i // PIECES, 1, i % PIECES).wait_recv()
        relay(i // PIECES, i % PIECES).wait_recv()
        return 0

    blank = jnp.zeros((16, white.shape[4]), jnp.bfloat16)

    def multiply(g, _):
        pieces = []
        for j in range(4):
            pieces += [white[j, w, g] for w in range(windows)] + [blank]
        found = jnp.dot(spread[g], jnp.concatenate(pieces, axis=0), preferred_element_type=jnp.float32)
        cross[:, g] = found.astype(jnp.bfloat16).reshape(used, 16, -1)
        return 0

    def lagged(s, half):
        part = cross[s, GROUPS // 2 * half : GROUPS // 2 * (half + 1)].reshape(BINS, -1)
        return jnp.dot(lags[:, BINS * half : BINS * (half + 1)], part, preferred_element_type=jnp.float32)

    def leave(s):
        return pltpu.make_async_copy(done.at[s], out.at[s], out_sem.at[s])

    def first_half(s, _):
        partial[s] = lagged(s, 0)
        return 0

    def second_half(s, _):
        done[s] = (partial[s] + lagged(s, 1)).astype(jnp.bfloat16)
        leave(s).start()
        return 0

    last = (windows - 1) * PIECES
    deal(1).wait_recv()
    build_half(0)
    consts[4].wait()
    lax.fori_loop(0, last, arrive, 0)
    forward(last, 0)

    def finish(i, _):
        w, p = i // PIECES, i % PIECES
        hand(w, 1, p).wait_send()
        hand(w, 2, p).wait_send()
        relay(w, p).wait_send()
        return 0

    def sent(w, _):
        def one(k, _):
            send(w, k).wait_send()
            return 0

        lax.fori_loop(1, blocks, one, 0, unroll=8)
        return 0

    lax.fori_loop(0, windows, sent, 0)
    lax.fori_loop(0, last, finish, 0)
    cast(0, 1).wait_send()
    for k in (1, 2, 3):
        cast(1, k).wait_send()
        cast(2, k).wait_send()
    for k in (2, 3):
        deal(k).wait_recv()
    build_half(1)
    for p in range(PIECES):
        if p + 1 < PIECES:
            forward(last + p + 1, 0)
        arrive(last + p, 0)
        lax.fori_loop(p * piece, (p + 1) * piece, multiply, 0, unroll=4)
        if p == PIECES // 2 - 1:
            lax.fori_loop(0, used, first_half, 0, unroll=2)
    lax.fori_loop(0, used, second_half, 0, unroll=2)

    for k in (1, 2, 3):
        deal(k).wait_send()
    lax.fori_loop(last, windows * PIECES, finish, 0)

    def left_all(s, _):
        leave(s).wait()
        return 0

    lax.fori_loop(0, used, left_all, 0)


def duplicate(source, target, held, load_sem, store_sem):
    loads = [pltpu.make_async_copy(source.at[i], held.at[i], load_sem.at[i]) for i in range(source.shape[0])]
    stores = [pltpu.make_async_copy(held.at[i], target.at[i], store_sem.at[i]) for i in range(source.shape[0])]
    for load in loads:
        load.start()
    for load, store in zip(loads, stores):
        load.wait()
        store.start()
    for store in stores:
        store.wait()


def body(record, offsets, sources):
    windows, count, channels = record.shape
    blocks, hosts = lax.axis_size("chan"), lax.axis_size("win")
    width = channels // blocks
    per = sources.shape[1] // hosts
    used = ROUNDS * per
    basis = jnp.asarray(np.concatenate(split_pair(sample_basis(count).T)))
    tables = jnp.asarray(spectrum_tables(count, blocks))
    scale = 1 / math.sqrt(windows * hosts * BINS)
    lags = jnp.asarray(lag_matrix(scale).astype(jnp.bfloat16))
    dma = pltpu.SemaphoreType.DMA
    anywhere = pl.BlockSpec(memory_space=pl.ANY)
    out = pl.pallas_call(
        exchange,
        out_shape=jax.ShapeDtypeStruct((used, LAGS, width), jnp.bfloat16),
        in_specs=[anywhere] * 6,
        out_specs=anywhere,
        scratch_shapes=[
            pltpu.VMEM((windows, 8, count, channels // 8), jnp.bfloat16),
            pltpu.VMEM(tables.shape, jnp.float32),
            pltpu.VMEM(basis.shape, jnp.bfloat16),
            pltpu.VMEM(lags.shape, jnp.bfloat16),
            pltpu.SMEM(offsets.shape, jnp.int32),
            pltpu.SMEM(sources.shape, jnp.int32),
            pltpu.VMEM((windows,) + basis.shape, jnp.bfloat16),
            pltpu.VMEM((BINS, 128), jnp.float32),
            pltpu.VMEM((windows, blocks, 16, 2 * width), jnp.bfloat16),
            pltpu.VMEM((windows, blocks, 16, 2 * width), jnp.bfloat16),
            pltpu.VMEM((windows, channels // 128, RANK, 128), jnp.bfloat16),
            pltpu.VMEM((4, 2, 4, windows, 16, 128), jnp.bfloat16),
            pltpu.VMEM((windows, 2, GROUPS, 16, blocks * RANK), jnp.bfloat16),
            pltpu.VMEM((2 * BINS, width), jnp.float32),
            pltpu.VMEM((GROUPS, 64, 128), jnp.float32),
            pltpu.VMEM((hosts, windows, GROUPS, 16, width), jnp.bfloat16),
            pltpu.VMEM((hosts, GROUPS // 2, SLOTS, 128), jnp.bfloat16),
            pltpu.VMEM((hosts, GROUPS // 2, SLOTS, 128), jnp.bfloat16),
            pltpu.VMEM((GROUPS, used * 16, 256), jnp.bfloat16),
            pltpu.VMEM((used, GROUPS, 16, width), jnp.bfloat16),
            pltpu.VMEM((used, LAGS, width), jnp.float32),
            pltpu.VMEM((used, LAGS, width), jnp.bfloat16),
            dma((windows, 8)),
            dma((5,)),
            dma((windows, blocks)),
            dma((windows, blocks)),
            dma((3, windows, PIECES)),
            dma((3, windows, PIECES)),
            dma((4,)),
            dma((4,)),
            dma((3, 4)),
            dma((3, 4)),
            dma((used,)),
        ],
        compiler_params=pltpu.CompilerParams(collective_id=0, has_side_effects=True, vmem_limit_bytes=56 << 20),
    )(record, tables, basis, lags, offsets, sources)
    out = pl.pallas_call(
        duplicate,
        out_shape=jax.ShapeDtypeStruct(out.shape, out.dtype),
        in_specs=[anywhere],
        out_specs=anywhere,
        scratch_shapes=[pltpu.VMEM(out.shape, out.dtype), dma((used,)), dma((used,))],
    )(out)
    return out.reshape(ROUNDS, per, LAGS, width)


def solution(mesh):
    return jax.shard_map(
        body,
        mesh=mesh,
        in_specs=(P("win", "chan", None), P("win"), P()),
        out_specs=P(None, "win", None, "chan"),
        check_vma=False,
    )
```

```python
import math

import jax
import jax.numpy as jnp
import numpy as np
from jax import lax
from jax.experimental import pallas as pl
from jax.experimental.pallas import tpu as pltpu
from jax.sharding import PartitionSpec as P

SAMPLES = 7680
BINS = 256
F0 = 16
LAGS = 256
LAG_STEP = 8
ROUNDS = 3
RANK = 32
GROUPS = BINS // 8
SLOTS = 16
PIECES = 4
EARLY = 1
MESH = pl.DeviceIdType.MESH


def sample_basis(count):
    half = (F0 + BINS) / SAMPLES
    at = np.arange(count)
    matrix = np.diag(((count - 1) / 2 - at) ** 2 * math.cos(2 * math.pi * half))
    side = at[1:] * (count - at[1:]) / 2
    matrix = matrix + np.diag(side, 1) + np.diag(side, -1)
    vectors = np.linalg.eigh(matrix)[1][:, ::-1][:, :RANK]
    return vectors * np.where(vectors[0] < 0, -1.0, 1.0)


def spectrum_tables(count, blocks):
    basis = sample_basis(count)
    middle = (count - 1) / 2
    at = np.arange(count) - middle
    terms = []
    for step, weight in ((0, 0.5), (1, -0.25), (-1, -0.25)):
        freqs = np.arange(BINS) + F0 + step
        wave = np.exp(-2j * math.pi / SAMPLES * np.outer(freqs, at)) @ basis
        turn = np.exp(-2j * math.pi / SAMPLES * np.outer(freqs, count * np.arange(blocks) + middle))
        table = weight * (turn[:, :, None] * wave[:, None, :]).reshape(BINS, blocks, 2, RANK // 2)
        terms.append(table.transpose(0, 2, 1, 3).reshape(BINS, blocks * RANK))
    own, above, below = terms
    return np.stack([p for t in (own, above + below, above - below) for p in (t.real, t.imag)]).astype(np.float32)


def lag_matrix(scale):
    shifts = LAG_STEP * (np.arange(LAGS) - LAGS // 2)
    phase = shifts[:, None] * (np.arange(BINS) + F0)[None, :] % SAMPLES
    angle = 2 * math.pi / SAMPLES * phase
    both = np.stack([np.cos(angle), np.sin(angle)], axis=1).reshape(LAGS, 2, GROUPS, 8)
    return (both.transpose(0, 2, 1, 3).reshape(LAGS, 2 * BINS) * scale).astype(np.float32)


def split_pair(array):
    high = array.astype(jnp.bfloat16)
    return high, (array - high.astype(array.dtype)).astype(jnp.bfloat16)


def exchange(
    record, tables, basis_in, lags_in, offsets_in, sources_in, out,
    held, parts, basis, lags, offsets, sources, masked, turns, message, arrived, coded, picked, full, spectra, columns,
    white, rows, rows_in, spread, cross, partial, done,
    load_sem, const_sem, send_sem, recv_sem, pass_sem, take_sem, rows_send, rows_recv, pick_send, pick_recv, out_sem,
):
    windows, chunks = held.shape[:2]
    blocks = message.shape[1]
    samples = held.shape[2]
    slots = sources.shape[1] // 4
    me, win = lax.axis_index("chan"), lax.axis_index("win")

    def load(w, k):
        at = (me // 4) ^ k
        source = record.at[w, :, pl.ds(pl.multiple_of(at * 1024, 1024), 1024)]
        return pltpu.make_async_copy(source, held.at[w, k], load_sem.at[w, k])

    def start_load(i, _):
        load(i // chunks, i % chunks).start()
        return 0

    lax.fori_loop(0, chunks, start_load, 0)
    pairs = ((offsets_in, offsets), (sources_in, sources), (basis_in, basis), (tables, parts), (lags_in, lags))
    consts = [pltpu.make_async_copy(a, b, const_sem.at[i]) for i, (a, b) in enumerate(pairs)]
    for copy in consts[:3]:
        copy.start()
    lax.fori_loop(chunks, windows * chunks, start_load, 0)
    for copy in consts[3:]:
        copy.start()

    barrier = pltpu.get_barrier_semaphore()

    def greet(k, _):
        pl.semaphore_signal(barrier, inc=1, device_id=(win, me ^ k), device_id_type=MESH)
        return 0

    lax.fori_loop(1, blocks, greet, 0)
    for k in (1, 2, 3):
        pl.semaphore_signal(barrier, inc=1, device_id=(win ^ k, me), device_id_type=MESH)

    for copy in consts[:3]:
        copy.wait()

    for w in range(windows):
        time = lax.broadcasted_iota(jnp.int32, basis.shape, 1) + (me * samples - offsets[w])
        inside = (time >= 0) & (time < SAMPLES)
        masked[w] = jnp.where(inside, basis[...].astype(jnp.float32), 0.0).astype(jnp.bfloat16)

    wide = lax.broadcasted_iota(jnp.int32, turns.shape, 1)
    freq = jnp.where(wide % 4 < 2, lax.broadcasted_iota(jnp.int32, turns.shape, 0) + F0, 1)
    shift = jnp.zeros(turns.shape, jnp.int32)
    for w in range(windows):
        shift = jnp.where(wide // 4 == w, offsets[w], shift)
    turn = (freq * shift).astype(jnp.float32)
    turn = turn - SAMPLES * jnp.floor(turn * (1 / SAMPLES))
    turn = turn * (2 * math.pi / SAMPLES) - jnp.where(wide % 2 == 1, math.pi / 2, 0.0)
    turns[...] = jnp.cos(turn)

    lane = lax.broadcasted_iota(jnp.int32, (16, 128), 1)
    columns[:, 48:, :] = jnp.zeros((GROUPS, 16, 128), jnp.float32)

    def project(w):
        def chunk(k, _):
            load(w, k).wait()
            at = (me // 4) ^ k
            found = jnp.dot(masked[w], held[w, k], preferred_element_type=jnp.float32)
            found = (found[:RANK] + found[RANK:]).astype(jnp.bfloat16)
            for i in range(4):
                part = found[:, 256 * i : 256 * (i + 1)]
                message[w, at * 4 + i, :, 0:256] = part[:16]
                message[w, at * 4 + i, :, 256:512] = part[16:]
            for i in range(8):
                coded[w, at * 8 + i] = found[:, 128 * i : 128 * (i + 1)]
            return 0

        lax.fori_loop(0, chunks, chunk, 0)

        arrived[w, me] = message[w, me]

    def choose(w, _):
        wide = lax.broadcasted_iota(jnp.int32, (RANK, 128), 1)

        def pick(i, total):
            slot = i // 12 * SLOTS + i % 12
            source = sources[i % 12 // slots, i // 12 * slots + i % slots]
            tile = coded[w, source // 128].astype(jnp.float32)
            value = jnp.sum(jnp.where(wide == source % 128, tile, 0.0), axis=1, keepdims=True)
            total = jnp.where(lane == slot, value[:16], total)
            return jnp.where(lane == slot + 64, value[16:], total)

        chosen = lax.fori_loop(0, ROUNDS * slots * 4, pick, jnp.zeros((16, 128), jnp.float32), unroll=8)
        picked[me // 8, me // 4 % 2, me % 4, w] = chosen.astype(jnp.bfloat16)
        return 0

    def cast(step, k):
        x, z, y = me // 8, me // 4 % 2, me % 4
        part = (picked.at[x, z, y], picked.at[x, :, y], picked.at[:, :, y])[step]
        return pltpu.make_async_remote_copy(
            part, part, pick_send.at[step, k], pick_recv.at[step, k],
            device_id=(win, me ^ (4, 8 * k, k)[step]), device_id_type=MESH,
        )

    def caught(step, k):
        there = me ^ (4, 8 * k, k)[step]
        x, z, y = there // 8, there // 4 % 2, there % 4
        part = (picked.at[x, z, y], picked.at[x, :, y], picked.at[:, :, y])[step]
        return pltpu.make_async_remote_copy(
            part, part, pick_send.at[step, k], pick_recv.at[step, k],
            device_id=(win, there), device_id_type=MESH,
        )

    def send(w, k):
        return pltpu.make_async_remote_copy(
            message.at[w, me ^ k], arrived.at[w, me], send_sem.at[w, k], recv_sem.at[w, me],
            device_id=(win, me ^ k), device_id_type=MESH,
        )

    def receive(w, k):
        return pltpu.make_async_remote_copy(
            message.at[w, me ^ k], arrived.at[w, me ^ k], send_sem.at[w, k], recv_sem.at[w, me ^ k],
            device_id=(win, me ^ k), device_id_type=MESH,
        )

    def start_sends(w):
        def one(k, _):
            send(w, k).start()
            return 0

        lax.fori_loop(1, blocks, one, 0, unroll=8)

    project(0)
    pl.semaphore_wait(barrier, blocks - 1 + 3)
    start_sends(0)
    project(1)
    start_sends(1)
    project(2)
    start_sends(2)
    lax.fori_loop(0, windows, choose, 0)
    cast(0, 1).start()

    consts[3].wait()

    def tabulate(w, g):
        own_re, own_im, sum_re, sum_im, dif_re, dif_im = [parts[t, pl.ds(pl.multiple_of(g * 8, 8), 8)] for t in range(6)]
        turn = turns[pl.ds(pl.multiple_of(g * 8, 8), 8), :][:, 4 * w : 4 * w + 4]
        c, s = turn[:, 2:3], turn[:, 3:4]
        re = own_re + c * sum_re - s * dif_im
        im = own_im + c * sum_im + s * dif_re
        c, s = turn[:, 0:1], turn[:, 1:2]
        both = jnp.concatenate([c * re - s * im, c * im + s * re], axis=0)
        high = both.astype(jnp.bfloat16)
        full[w, 0, g] = high
        full[w, 1, g] = (both - high.astype(jnp.float32)).astype(jnp.bfloat16)
        return 0

    for w in range(windows):
        lax.fori_loop(0, GROUPS, lambda g, _, w=w: tabulate(w, g), 0, unroll=4)

    piece = GROUPS // PIECES

    def hand(w, k, p):
        part = pl.ds(p * piece, piece)
        return pltpu.make_async_remote_copy(
            white.at[0, w, part], white.at[k, w, part], pass_sem.at[k - 1, w, p], take_sem.at[k - 1, w, p],
            device_id=(win ^ k, me), device_id_type=MESH,
        )

    def relay(w, p):
        part = pl.ds(p * piece, piece)
        return pltpu.make_async_remote_copy(
            white.at[2, w, part], white.at[3, w, part], pass_sem.at[2, w, p], take_sem.at[2, w, p],
            device_id=(win ^ 1, me), device_id_type=MESH,
        )

    def whiten(w):
        def wait_one(k, _):
            receive(w, k).wait_recv()
            return 0

        lax.fori_loop(1, blocks, wait_one, 0, unroll=8)
        first = arrived[w, :, :, 0:256].reshape(blocks * 16, 256)
        second = arrived[w, :, :, 256:512].reshape(blocks * 16, 256)
        cut = blocks * 16

        def tile(m, power):
            found = jnp.zeros((128, 256), jnp.float32)
            for half in range(2):
                table = full[w, half, pl.ds(m * 8, 8)].reshape(128, 2 * cut)
                found += jnp.dot(table[:, :cut], first, preferred_element_type=jnp.float32)
                found += jnp.dot(table[:, cut:], second, preferred_element_type=jnp.float32)
            spectra[pl.ds(pl.multiple_of(m * 128, 128), 128)] = found
            return power + jnp.sum(found * found, axis=0, keepdims=True)

        power = lax.fori_loop(0, 4, tile, jnp.zeros((1, 256), jnp.float32))
        scale = lax.rsqrt(power * (1 / (2 * BINS)) + 1e-06)

        def norm(m, _):
            found = (spectra[pl.ds(pl.multiple_of(m * 128, 128), 128)] * scale).astype(jnp.bfloat16)
            white[0, w, pl.ds(m * 8, 8)] = found.reshape(8, 16, 256)
            return 0

        lax.fori_loop(0, 4, norm, 0, unroll=2)
        for p in range(PIECES if w < windows - 1 else EARLY):
            hand(w, 2, p).start()
        for p in range(PIECES if w < windows - 1 else EARLY):
            hand(w, 1, p).start()

    def whiten_picked(w, _):
        extra = picked[:, :, :, w].reshape(blocks * 16, 128)
        cut = blocks * 16

        def tile(m, power):
            low = jnp.zeros((128, 128), jnp.float32)
            top = jnp.zeros((128, 128), jnp.float32)
            for half in range(1):
                table = full[w, half, pl.ds(m * 8, 8)].reshape(128, 2 * cut)
                low += jnp.dot(table[:, :cut], extra, preferred_element_type=jnp.float32)
                top += jnp.dot(table[:, cut:], extra, preferred_element_type=jnp.float32)
            found = low + pltpu.roll(top, 64, 1)
            spectra[pl.ds(pl.multiple_of(m * 128, 128), 128), 0:128] = found
            return power + jnp.sum(found * found, axis=0, keepdims=True)

        power = lax.fori_loop(0, 4, tile, jnp.zeros((1, 128), jnp.float32))
        scale = lax.rsqrt(power * (1 / (2 * BINS)) + 1e-06)

        def norm(m, _):
            found = spectra[pl.ds(pl.multiple_of(m * 128, 128), 128), 0:128] * scale
            columns[pl.ds(m * 8, 8), pl.ds(pl.multiple_of(w * 16, 16), 16)] = (
                found.astype(jnp.bfloat16).astype(jnp.float32).reshape(8, 16, 128)
            )
            return 0

        lax.fori_loop(0, 4, norm, 0, unroll=2)
        return 0

    caught(0, 1).wait_recv()
    for k in (2, 1, 3):
        cast(1, k).start()
    whiten(0)
    for k in (1, 2, 3):
        caught(1, k).wait_recv()
    for k in (2, 1, 3):
        cast(2, k).start()
    whiten(1)
    whiten(2)
    for k in (1, 2, 3):
        caught(2, k).wait_recv()
    lax.fori_loop(0, windows, whiten_picked, 0)

    def turn_over(at, _):
        block = columns[pl.ds(at * 2, 2)].reshape(128, 128).T
        rows[:, at] = block[:64].reshape(4, SLOTS, 128).astype(jnp.bfloat16)
        return 0

    lax.fori_loop(0, GROUPS // 2, turn_over, 0, unroll=4)

    def deal(k):
        return pltpu.make_async_remote_copy(
            rows.at[win ^ k], rows_in.at[k], rows_send.at[k], rows_recv.at[k],
            device_id=(win ^ k, me), device_id_type=MESH,
        )

    for k in (2, 3, 1):
        deal(k).start()
    for p in range(EARLY, PIECES):
        hand(windows - 1, 2, p).start()
        hand(windows - 1, 1, p).start()
    rows_in[0] = rows[win]

    def forward(i, _):
        hand(i // PIECES, 2, i % PIECES).wait_recv()
        relay(i // PIECES, i % PIECES).start()
        return 0

    lax.fori_loop(0, (windows - 1) * PIECES, forward, 0)
    lane = lax.broadcasted_iota(jnp.int32, (SLOTS, 128), 1)
    left = lane < 64
    real = lane % 16 < 8
    own = lax.broadcasted_iota(jnp.int32, (8, 128), 1) % 8 == lax.broadcasted_iota(jnp.int32, (8, 128), 0)
    own = jnp.where(own, 1.0, 0.0).astype(jnp.float32)
    used = done.shape[0]

    def build(at, half):
        tiles = [rows_in[2 * half + j, at].astype(jnp.float32) for j in range(2)]
        for odd in range(2):
            if odd:
                both = jnp.where(left, pltpu.roll(tiles[0], 64, 1), tiles[1])
            else:
                both = jnp.where(left, tiles[0], pltpu.roll(tiles[1], 64, 1))
            turned = jnp.where(real, pltpu.roll(both, 120, 1), -pltpu.roll(both, 8, 1))
            table = jnp.stack([both[:used, None, :] * own[None], turned[:used, None, :] * own[None]], axis=1)
            spread[at * 2 + odd, :, 128 * half : 128 * (half + 1)] = table.reshape(used * 16, 128).astype(jnp.bfloat16)

    def build_half(half):
        def one(at, _):
            build(at, half)
            return 0

        lax.fori_loop(0, GROUPS // 2, one, 0, unroll=4)

    def arrive(i, _):
        hand(i // PIECES, 1, i % PIECES).wait_recv()
        relay(i // PIECES, i % PIECES).wait_recv()
        return 0

    blank = jnp.zeros((16, white.shape[4]), jnp.bfloat16)

    def multiply(g, _):
        pieces = []
        for j in range(4):
            pieces += [white[j, w, g] for w in range(windows)] + [blank]
        found = jnp.dot(spread[g], jnp.concatenate(pieces, axis=0), preferred_element_type=jnp.float32)
        cross[:, g] = found.astype(jnp.bfloat16).reshape(used, 16, -1)
        return 0

    def lagged(s, half):
        part = cross[s, GROUPS // 2 * half : GROUPS // 2 * (half + 1)].reshape(BINS, -1)
        return jnp.dot(lags[:, BINS * half : BINS * (half + 1)], part, preferred_element_type=jnp.float32)

    def leave(s):
        return pltpu.make_async_copy(done.at[s], out.at[s], out_sem.at[s])

    def first_half(s, _):
        partial[s] = lagged(s, 0)
        return 0

    def second_half(s, _):
        done[s] = (partial[s] + lagged(s, 1)).astype(jnp.bfloat16)
        leave(s).start()
        return 0

    last = (windows - 1) * PIECES
    deal(1).wait_recv()
    build_half(0)
    consts[4].wait()
    lax.fori_loop(0, last, arrive, 0)
    forward(last, 0)

    def finish(i, _):
        w, p = i // PIECES, i % PIECES
        hand(w, 1, p).wait_send()
        hand(w, 2, p).wait_send()
        relay(w, p).wait_send()
        return 0

    def sent(w, _):
        def one(k, _):
            send(w, k).wait_send()
            return 0

        lax.fori_loop(1, blocks, one, 0, unroll=8)
        return 0

    lax.fori_loop(0, windows, sent, 0)
    lax.fori_loop(0, last, finish, 0)
    cast(0, 1).wait_send()
    for k in (1, 2, 3):
        cast(1, k).wait_send()
        cast(2, k).wait_send()
    for k in (2, 3):
        deal(k).wait_recv()
    build_half(1)
    for p in range(PIECES):
        if p + 1 < PIECES:
            forward(last + p + 1, 0)
        arrive(last + p, 0)
        lax.fori_loop(p * piece, (p + 1) * piece, multiply, 0, unroll=4)
        if p == PIECES // 2 - 1:
            lax.fori_loop(0, used, first_half, 0, unroll=2)
    lax.fori_loop(0, used, second_half, 0, unroll=2)

    for k in (1, 2, 3):
        deal(k).wait_send()
    lax.fori_loop(last, windows * PIECES, finish, 0)

    def left_all(s, _):
        leave(s).wait()
        return 0

    lax.fori_loop(0, used, left_all, 0)


def duplicate(source, target, held, load_sem, store_sem):
    loads = [pltpu.make_async_copy(source.at[i], held.at[i], load_sem.at[i]) for i in range(source.shape[0])]
    stores = [pltpu.make_async_copy(held.at[i], target.at[i], store_sem.at[i]) for i in range(source.shape[0])]
    for load in loads:
        load.start()
    for load, store in zip(loads, stores):
        load.wait()
        store.start()
    for store in stores:
        store.wait()


def body(record, offsets, sources):
    windows, count, channels = record.shape
    blocks, hosts = lax.axis_size("chan"), lax.axis_size("win")
    width = channels // blocks
    per = sources.shape[1] // hosts
    used = ROUNDS * per
    basis = jnp.asarray(np.concatenate(split_pair(sample_basis(count).T)))
    tables = jnp.asarray(spectrum_tables(count, blocks))
    scale = 1 / math.sqrt(windows * hosts * BINS)
    lags = jnp.asarray(lag_matrix(scale).astype(jnp.bfloat16))
    dma = pltpu.SemaphoreType.DMA
    anywhere = pl.BlockSpec(memory_space=pl.ANY)
    out = pl.pallas_call(
        exchange,
        out_shape=jax.ShapeDtypeStruct((used, LAGS, width), jnp.bfloat16),
        in_specs=[anywhere] * 6,
        out_specs=anywhere,
        scratch_shapes=[
            pltpu.VMEM((windows, 8, count, channels // 8), jnp.bfloat16),
            pltpu.VMEM(tables.shape, jnp.float32),
            pltpu.VMEM(basis.shape, jnp.bfloat16),
            pltpu.VMEM(lags.shape, jnp.bfloat16),
            pltpu.SMEM(offsets.shape, jnp.int32),
            pltpu.SMEM(sources.shape, jnp.int32),
            pltpu.VMEM((windows,) + basis.shape, jnp.bfloat16),
            pltpu.VMEM((BINS, 128), jnp.float32),
            pltpu.VMEM((windows, blocks, 16, 2 * width), jnp.bfloat16),
            pltpu.VMEM((windows, blocks, 16, 2 * width), jnp.bfloat16),
            pltpu.VMEM((windows, channels // 128, RANK, 128), jnp.bfloat16),
            pltpu.VMEM((4, 2, 4, windows, 16, 128), jnp.bfloat16),
            pltpu.VMEM((windows, 2, GROUPS, 16, blocks * RANK), jnp.bfloat16),
            pltpu.VMEM((2 * BINS, width), jnp.float32),
            pltpu.VMEM((GROUPS, 64, 128), jnp.float32),
            pltpu.VMEM((hosts, windows, GROUPS, 16, width), jnp.bfloat16),
            pltpu.VMEM((hosts, GROUPS // 2, SLOTS, 128), jnp.bfloat16),
            pltpu.VMEM((hosts, GROUPS // 2, SLOTS, 128), jnp.bfloat16),
            pltpu.VMEM((GROUPS, used * 16, 256), jnp.bfloat16),
            pltpu.VMEM((used, GROUPS, 16, width), jnp.bfloat16),
            pltpu.VMEM((used, LAGS, width), jnp.float32),
            pltpu.VMEM((used, LAGS, width), jnp.bfloat16),
            dma((windows, 8)),
            dma((5,)),
            dma((windows, blocks)),
            dma((windows, blocks)),
            dma((3, windows, PIECES)),
            dma((3, windows, PIECES)),
            dma((4,)),
            dma((4,)),
            dma((3, 4)),
            dma((3, 4)),
            dma((used,)),
        ],
        compiler_params=pltpu.CompilerParams(collective_id=0, has_side_effects=True, vmem_limit_bytes=56 << 20),
    )(record, tables, basis, lags, offsets, sources)
    out = pl.pallas_call(
        duplicate,
        out_shape=jax.ShapeDtypeStruct(out.shape, out.dtype),
        in_specs=[anywhere],
        out_specs=anywhere,
        scratch_shapes=[pltpu.VMEM(out.shape, out.dtype), dma((used,)), dma((used,))],
    )(out)
    return out.reshape(ROUNDS, per, LAGS, width)


def solution(mesh):
    return jax.shard_map(
        body,
        mesh=mesh,
        in_specs=(P("win", "chan", None), P("win"), P()),
        out_specs=P(None, "win", None, "chan"),
        check_vma=False,
    )
```

```python
import math

import jax
import jax.numpy as jnp
import numpy as np
from jax import lax
from jax.experimental import pallas as pl
from jax.experimental.pallas import tpu as pltpu
from jax.sharding import PartitionSpec as P

SAMPLES = 7680
BINS = 256
F0 = 16
LAGS = 256
LAG_STEP = 8
ROUNDS = 3
RANK = 32
GROUPS = BINS // 8
SLOTS = 16
PIECES = 4
EARLY = 1
MESH = pl.DeviceIdType.MESH


def sample_basis(count):
    half = (F0 + BINS) / SAMPLES
    at = np.arange(count)
    matrix = np.diag(((count - 1) / 2 - at) ** 2 * math.cos(2 * math.pi * half))
    side = at[1:] * (count - at[1:]) / 2
    matrix = matrix + np.diag(side, 1) + np.diag(side, -1)
    vectors = np.linalg.eigh(matrix)[1][:, ::-1][:, :RANK]
    return vectors * np.where(vectors[0] < 0, -1.0, 1.0)


def spectrum_tables(count, blocks):
    basis = sample_basis(count)
    middle = (count - 1) / 2
    at = np.arange(count) - middle
    terms = []
    for step, weight in ((0, 0.5), (1, -0.25), (-1, -0.25)):
        freqs = np.arange(BINS) + F0 + step
        wave = np.exp(-2j * math.pi / SAMPLES * np.outer(freqs, at)) @ basis
        turn = np.exp(-2j * math.pi / SAMPLES * np.outer(freqs, count * np.arange(blocks) + middle))
        table = weight * (turn[:, :, None] * wave[:, None, :]).reshape(BINS, blocks, 2, RANK // 2)
        terms.append(table.transpose(0, 2, 1, 3).reshape(BINS, blocks * RANK))
    own, above, below = terms
    return np.stack([p for t in (own, above + below, above - below) for p in (t.real, t.imag)]).astype(np.float32)


def lag_matrix(scale):
    shifts = LAG_STEP * (np.arange(LAGS) - LAGS // 2)
    phase = shifts[:, None] * (np.arange(BINS) + F0)[None, :] % SAMPLES
    angle = 2 * math.pi / SAMPLES * phase
    both = np.stack([np.cos(angle), np.sin(angle)], axis=1).reshape(LAGS, 2, GROUPS, 8)
    return (both.transpose(0, 2, 1, 3).reshape(LAGS, 2 * BINS) * scale).astype(np.float32)


def split_pair(array):
    high = array.astype(jnp.bfloat16)
    return high, (array - high.astype(array.dtype)).astype(jnp.bfloat16)


def exchange(
    record, tables, basis_in, lags_in, offsets_in, sources_in, out,
    held, parts, basis, lags, offsets, sources, masked, turns, message, arrived, coded, picked, full, spectra, columns,
    white, rows, rows_in, spread, cross, partial, done,
    load_sem, const_sem, send_sem, recv_sem, pass_sem, take_sem, rows_send, rows_recv, pick_send, pick_recv, out_sem,
):
    windows, chunks = held.shape[:2]
    blocks = message.shape[1]
    samples = held.shape[2]
    slots = sources.shape[1] // 4
    me, win = lax.axis_index("chan"), lax.axis_index("win")

    def load(w, k):
        at = (me // 4) ^ k
        source = record.at[w, :, pl.ds(pl.multiple_of(at * 1024, 1024), 1024)]
        return pltpu.make_async_copy(source, held.at[w, k], load_sem.at[w, k])

    def start_load(i, _):
        load(i // chunks, i % chunks).start()
        return 0

    lax.fori_loop(0, chunks, start_load, 0)
    pairs = ((offsets_in, offsets), (sources_in, sources), (basis_in, basis), (tables, parts), (lags_in, lags))
    consts = [pltpu.make_async_copy(a, b, const_sem.at[i]) for i, (a, b) in enumerate(pairs)]
    for copy in consts[:3]:
        copy.start()
    lax.fori_loop(chunks, windows * chunks, start_load, 0)
    for copy in consts[3:]:
        copy.start()

    barrier = pltpu.get_barrier_semaphore()

    def greet(k, _):
        pl.semaphore_signal(barrier, inc=1, device_id=(win, me ^ k), device_id_type=MESH)
        return 0

    lax.fori_loop(1, blocks, greet, 0)
    for k in (1, 2, 3):
        pl.semaphore_signal(barrier, inc=1, device_id=(win ^ k, me), device_id_type=MESH)

    for copy in consts[:3]:
        copy.wait()

    for w in range(windows):
        time = lax.broadcasted_iota(jnp.int32, basis.shape, 1) + (me * samples - offsets[w])
        inside = (time >= 0) & (time < SAMPLES)
        masked[w] = jnp.where(inside, basis[...].astype(jnp.float32), 0.0).astype(jnp.bfloat16)

    wide = lax.broadcasted_iota(jnp.int32, turns.shape, 1)
    freq = jnp.where(wide % 4 < 2, lax.broadcasted_iota(jnp.int32, turns.shape, 0) + F0, 1)
    shift = jnp.zeros(turns.shape, jnp.int32)
    for w in range(windows):
        shift = jnp.where(wide // 4 == w, offsets[w], shift)
    turn = (freq * shift).astype(jnp.float32)
    turn = turn - SAMPLES * jnp.floor(turn * (1 / SAMPLES))
    turn = turn * (2 * math.pi / SAMPLES) - jnp.where(wide % 2 == 1, math.pi / 2, 0.0)
    turns[...] = jnp.cos(turn)

    lane = lax.broadcasted_iota(jnp.int32, (16, 128), 1)
    columns[:, 48:, :] = jnp.zeros((GROUPS, 16, 128), jnp.float32)

    def project(w):
        def chunk(k, _):
            load(w, k).wait()
            at = (me // 4) ^ k
            found = jnp.dot(masked[w], held[w, k], preferred_element_type=jnp.float32)
            found = (found[:RANK] + found[RANK:]).astype(jnp.bfloat16)
            for i in range(4):
                part = found[:, 256 * i : 256 * (i + 1)]
                message[w, at * 4 + i, :, 0:256] = part[:16]
                message[w, at * 4 + i, :, 256:512] = part[16:]
            for i in range(8):
                coded[w, at * 8 + i] = found[:, 128 * i : 128 * (i + 1)]
            return 0

        lax.fori_loop(0, chunks, chunk, 0)

        arrived[w, me] = message[w, me]

    def choose(w, _):
        wide = lax.broadcasted_iota(jnp.int32, (RANK, 128), 1)

        def pick(i, total):
            slot = i // 12 * SLOTS + i % 12
            source = sources[i % 12 // slots, i // 12 * slots + i % slots]
            tile = coded[w, source // 128].astype(jnp.float32)
            value = jnp.sum(jnp.where(wide == source % 128, tile, 0.0), axis=1, keepdims=True)
            total = jnp.where(lane == slot, value[:16], total)
            return jnp.where(lane == slot + 64, value[16:], total)

        chosen = lax.fori_loop(0, ROUNDS * slots * 4, pick, jnp.zeros((16, 128), jnp.float32), unroll=8)
        picked[me // 8, me // 4 % 2, me % 4, w] = chosen.astype(jnp.bfloat16)
        return 0

    def cast(step, k):
        x, z, y = me // 8, me // 4 % 2, me % 4
        part = (picked.at[x, z, y], picked.at[x, :, y], picked.at[:, :, y])[step]
        return pltpu.make_async_remote_copy(
            part, part, pick_send.at[step, k], pick_recv.at[step, k],
            device_id=(win, me ^ (4, 8 * k, k)[step]), device_id_type=MESH,
        )

    def caught(step, k):
        there = me ^ (4, 8 * k, k)[step]
        x, z, y = there // 8, there // 4 % 2, there % 4
        part = (picked.at[x, z, y], picked.at[x, :, y], picked.at[:, :, y])[step]
        return pltpu.make_async_remote_copy(
            part, part, pick_send.at[step, k], pick_recv.at[step, k],
            device_id=(win, there), device_id_type=MESH,
        )

    def send(w, k):
        return pltpu.make_async_remote_copy(
            message.at[w, me ^ k], arrived.at[w, me], send_sem.at[w, k], recv_sem.at[w, me],
            device_id=(win, me ^ k), device_id_type=MESH,
        )

    def receive(w, k):
        return pltpu.make_async_remote_copy(
            message.at[w, me ^ k], arrived.at[w, me ^ k], send_sem.at[w, k], recv_sem.at[w, me ^ k],
            device_id=(win, me ^ k), device_id_type=MESH,
        )

    def start_sends(w):
        def one(k, _):
            send(w, k).start()
            return 0

        lax.fori_loop(1, blocks, one, 0, unroll=8)

    project(0)
    pl.semaphore_wait(barrier, blocks - 1 + 3)
    start_sends(0)
    project(1)
    start_sends(1)
    project(2)
    start_sends(2)
    lax.fori_loop(0, windows, choose, 0)
    cast(0, 1).start()

    consts[3].wait()

    def tabulate(w, g):
        own_re, own_im, sum_re, sum_im, dif_re, dif_im = [parts[t, pl.ds(pl.multiple_of(g * 8, 8), 8)] for t in range(6)]
        turn = turns[pl.ds(pl.multiple_of(g * 8, 8), 8), :][:, 4 * w : 4 * w + 4]
        c, s = turn[:, 2:3], turn[:, 3:4]
        re = own_re + c * sum_re - s * dif_im
        im = own_im + c * sum_im + s * dif_re
        c, s = turn[:, 0:1], turn[:, 1:2]
        both = jnp.concatenate([c * re - s * im, c * im + s * re], axis=0)
        high = both.astype(jnp.bfloat16)
        full[w, 0, g] = high
        full[w, 1, g] = (both - high.astype(jnp.float32)).astype(jnp.bfloat16)
        return 0


    piece = GROUPS // PIECES

    def hand(w, k, p):
        part = pl.ds(p * piece, piece)
        return pltpu.make_async_remote_copy(
            white.at[0, w, part], white.at[k, w, part], pass_sem.at[k - 1, w, p], take_sem.at[k - 1, w, p],
            device_id=(win ^ k, me), device_id_type=MESH,
        )

    def relay(w, p):
        part = pl.ds(p * piece, piece)
        return pltpu.make_async_remote_copy(
            white.at[2, w, part], white.at[3, w, part], pass_sem.at[2, w, p], take_sem.at[2, w, p],
            device_id=(win ^ 1, me), device_id_type=MESH,
        )

    def whiten(w):
        def wait_one(k, _):
            receive(w, k).wait_recv()
            return 0

        lax.fori_loop(1, blocks, wait_one, 0, unroll=8)
        first = arrived[w, :, :, 0:256].reshape(blocks * 16, 256)
        second = arrived[w, :, :, 256:512].reshape(blocks * 16, 256)
        cut = blocks * 16

        def tile(m, power):
            found = jnp.zeros((128, 256), jnp.float32)
            for half in range(2):
                table = full[w, half, pl.ds(m * 8, 8)].reshape(128, 2 * cut)
                found += jnp.dot(table[:, :cut], first, preferred_element_type=jnp.float32)
                found += jnp.dot(table[:, cut:], second, preferred_element_type=jnp.float32)
            spectra[pl.ds(pl.multiple_of(m * 128, 128), 128)] = found
            return power + jnp.sum(found * found, axis=0, keepdims=True)

        power = lax.fori_loop(0, 4, tile, jnp.zeros((1, 256), jnp.float32))
        scale = lax.rsqrt(power * (1 / (2 * BINS)) + 1e-06)

        def norm(m, _):
            found = (spectra[pl.ds(pl.multiple_of(m * 128, 128), 128)] * scale).astype(jnp.bfloat16)
            white[0, w, pl.ds(m * 8, 8)] = found.reshape(8, 16, 256)
            return 0

        lax.fori_loop(0, 4, norm, 0, unroll=2)
        for p in range(PIECES if w < windows - 1 else EARLY):
            hand(w, 2, p).start()
        for p in range(PIECES if w < windows - 1 else EARLY):
            hand(w, 1, p).start()

    def whiten_picked(w, _):
        extra = picked[:, :, :, w].reshape(blocks * 16, 128)
        cut = blocks * 16

        def tile(m, power):
            low = jnp.zeros((128, 128), jnp.float32)
            top = jnp.zeros((128, 128), jnp.float32)
            for half in range(1):
                table = full[w, half, pl.ds(m * 8, 8)].reshape(128, 2 * cut)
                low += jnp.dot(table[:, :cut], extra, preferred_element_type=jnp.float32)
                top += jnp.dot(table[:, cut:], extra, preferred_element_type=jnp.float32)
            found = low + pltpu.roll(top, 64, 1)
            spectra[pl.ds(pl.multiple_of(m * 128, 128), 128), 0:128] = found
            return power + jnp.sum(found * found, axis=0, keepdims=True)

        power = lax.fori_loop(0, 4, tile, jnp.zeros((1, 128), jnp.float32))
        scale = lax.rsqrt(power * (1 / (2 * BINS)) + 1e-06)

        def norm(m, _):
            found = spectra[pl.ds(pl.multiple_of(m * 128, 128), 128), 0:128] * scale
            columns[pl.ds(m * 8, 8), pl.ds(pl.multiple_of(w * 16, 16), 16)] = (
                found.astype(jnp.bfloat16).astype(jnp.float32).reshape(8, 16, 128)
            )
            return 0

        lax.fori_loop(0, 4, norm, 0, unroll=2)
        return 0

    lax.fori_loop(0, GROUPS, lambda g, _: tabulate(0, g), 0, unroll=4)
    caught(0, 1).wait_recv()
    for k in (2, 1, 3):
        cast(1, k).start()
    whiten(0)
    lax.fori_loop(0, GROUPS, lambda g, _: tabulate(1, g), 0, unroll=4)
    for k in (1, 2, 3):
        caught(1, k).wait_recv()
    for k in (2, 1, 3):
        cast(2, k).start()
    whiten(1)
    lax.fori_loop(0, GROUPS, lambda g, _: tabulate(2, g), 0, unroll=4)
    whiten(2)
    for k in (1, 2, 3):
        caught(2, k).wait_recv()
    lax.fori_loop(0, windows, whiten_picked, 0)

    def turn_over(at, _):
        block = columns[pl.ds(at * 2, 2)].reshape(128, 128).T
        rows[:, at] = block[:64].reshape(4, SLOTS, 128).astype(jnp.bfloat16)
        return 0

    lax.fori_loop(0, GROUPS // 2, turn_over, 0, unroll=4)

    def deal(k):
        return pltpu.make_async_remote_copy(
            rows.at[win ^ k], rows_in.at[k], rows_send.at[k], rows_recv.at[k],
            device_id=(win ^ k, me), device_id_type=MESH,
        )

    for k in (2, 3, 1):
        deal(k).start()
    for p in range(EARLY, PIECES):
        hand(windows - 1, 2, p).start()
        hand(windows - 1, 1, p).start()
    rows_in[0] = rows[win]

    def forward(i, _):
        hand(i // PIECES, 2, i % PIECES).wait_recv()
        relay(i // PIECES, i % PIECES).start()
        return 0

    lax.fori_loop(0, (windows - 1) * PIECES, forward, 0)
    lane = lax.broadcasted_iota(jnp.int32, (SLOTS, 128), 1)
    left = lane < 64
    real = lane % 16 < 8
    own = lax.broadcasted_iota(jnp.int32, (8, 128), 1) % 8 == lax.broadcasted_iota(jnp.int32, (8, 128), 0)
    own = jnp.where(own, 1.0, 0.0).astype(jnp.float32)
    used = done.shape[0]

    def build(at, half):
        tiles = [rows_in[2 * half + j, at].astype(jnp.float32) for j in range(2)]
        for odd in range(2):
            if odd:
                both = jnp.where(left, pltpu.roll(tiles[0], 64, 1), tiles[1])
            else:
                both = jnp.where(left, tiles[0], pltpu.roll(tiles[1], 64, 1))
            turned = jnp.where(real, pltpu.roll(both, 120, 1), -pltpu.roll(both, 8, 1))
            table = jnp.stack([both[:used, None, :] * own[None], turned[:used, None, :] * own[None]], axis=1)
            spread[at * 2 + odd, :, 128 * half : 128 * (half + 1)] = table.reshape(used * 16, 128).astype(jnp.bfloat16)

    def build_half(half):
        def one(at, _):
            build(at, half)
            return 0

        lax.fori_loop(0, GROUPS // 2, one, 0, unroll=4)

    def arrive(i, _):
        hand(i // PIECES, 1, i % PIECES).wait_recv()
        relay(i // PIECES, i % PIECES).wait_recv()
        return 0

    blank = jnp.zeros((16, white.shape[4]), jnp.bfloat16)

    def multiply(g, _):
        pieces = []
        for j in range(4):
            pieces += [white[j, w, g] for w in range(windows)] + [blank]
        found = jnp.dot(spread[g], jnp.concatenate(pieces, axis=0), preferred_element_type=jnp.float32)
        cross[:, g] = found.astype(jnp.bfloat16).reshape(used, 16, -1)
        return 0

    def lagged(s, half):
        part = cross[s, GROUPS // 2 * half : GROUPS // 2 * (half + 1)].reshape(BINS, -1)
        return jnp.dot(lags[:, BINS * half : BINS * (half + 1)], part, preferred_element_type=jnp.float32)

    def leave(s):
        return pltpu.make_async_copy(done.at[s], out.at[s], out_sem.at[s])

    def first_half(s, _):
        partial[s] = lagged(s, 0)
        return 0

    def second_half(s, _):
        done[s] = (partial[s] + lagged(s, 1)).astype(jnp.bfloat16)
        leave(s).start()
        return 0

    last = (windows - 1) * PIECES
    deal(1).wait_recv()
    build_half(0)
    consts[4].wait()
    lax.fori_loop(0, last, arrive, 0)
    forward(last, 0)

    def finish(i, _):
        w, p = i // PIECES, i % PIECES
        hand(w, 1, p).wait_send()
        hand(w, 2, p).wait_send()
        relay(w, p).wait_send()
        return 0

    def sent(w, _):
        def one(k, _):
            send(w, k).wait_send()
            return 0

        lax.fori_loop(1, blocks, one, 0, unroll=8)
        return 0

    lax.fori_loop(0, windows, sent, 0)
    lax.fori_loop(0, last, finish, 0)
    cast(0, 1).wait_send()
    for k in (1, 2, 3):
        cast(1, k).wait_send()
        cast(2, k).wait_send()
    for k in (2, 3):
        deal(k).wait_recv()
    build_half(1)
    for p in range(PIECES):
        if p + 1 < PIECES:
            forward(last + p + 1, 0)
        arrive(last + p, 0)
        lax.fori_loop(p * piece, (p + 1) * piece, multiply, 0, unroll=4)
        if p == PIECES // 2 - 1:
            lax.fori_loop(0, used, first_half, 0, unroll=2)
    lax.fori_loop(0, used, second_half, 0, unroll=2)

    for k in (1, 2, 3):
        deal(k).wait_send()
    lax.fori_loop(last, windows * PIECES, finish, 0)

    def left_all(s, _):
        leave(s).wait()
        return 0

    lax.fori_loop(0, used, left_all, 0)


def duplicate(source, target, held, load_sem, store_sem):
    loads = [pltpu.make_async_copy(source.at[i], held.at[i], load_sem.at[i]) for i in range(source.shape[0])]
    stores = [pltpu.make_async_copy(held.at[i], target.at[i], store_sem.at[i]) for i in range(source.shape[0])]
    for load in loads:
        load.start()
    for load, store in zip(loads, stores):
        load.wait()
        store.start()
    for store in stores:
        store.wait()


def body(record, offsets, sources):
    windows, count, channels = record.shape
    blocks, hosts = lax.axis_size("chan"), lax.axis_size("win")
    width = channels // blocks
    per = sources.shape[1] // hosts
    used = ROUNDS * per
    basis = jnp.asarray(np.concatenate(split_pair(sample_basis(count).T)))
    tables = jnp.asarray(spectrum_tables(count, blocks))
    scale = 1 / math.sqrt(windows * hosts * BINS)
    lags = jnp.asarray(lag_matrix(scale).astype(jnp.bfloat16))
    dma = pltpu.SemaphoreType.DMA
    anywhere = pl.BlockSpec(memory_space=pl.ANY)
    out = pl.pallas_call(
        exchange,
        out_shape=jax.ShapeDtypeStruct((used, LAGS, width), jnp.bfloat16),
        in_specs=[anywhere] * 6,
        out_specs=anywhere,
        scratch_shapes=[
            pltpu.VMEM((windows, 8, count, channels // 8), jnp.bfloat16),
            pltpu.VMEM(tables.shape, jnp.float32),
            pltpu.VMEM(basis.shape, jnp.bfloat16),
            pltpu.VMEM(lags.shape, jnp.bfloat16),
            pltpu.SMEM(offsets.shape, jnp.int32),
            pltpu.SMEM(sources.shape, jnp.int32),
            pltpu.VMEM((windows,) + basis.shape, jnp.bfloat16),
            pltpu.VMEM((BINS, 128), jnp.float32),
            pltpu.VMEM((windows, blocks, 16, 2 * width), jnp.bfloat16),
            pltpu.VMEM((windows, blocks, 16, 2 * width), jnp.bfloat16),
            pltpu.VMEM((windows, channels // 128, RANK, 128), jnp.bfloat16),
            pltpu.VMEM((4, 2, 4, windows, 16, 128), jnp.bfloat16),
            pltpu.VMEM((windows, 2, GROUPS, 16, blocks * RANK), jnp.bfloat16),
            pltpu.VMEM((2 * BINS, width), jnp.float32),
            pltpu.VMEM((GROUPS, 64, 128), jnp.float32),
            pltpu.VMEM((hosts, windows, GROUPS, 16, width), jnp.bfloat16),
            pltpu.VMEM((hosts, GROUPS // 2, SLOTS, 128), jnp.bfloat16),
            pltpu.VMEM((hosts, GROUPS // 2, SLOTS, 128), jnp.bfloat16),
            pltpu.VMEM((GROUPS, used * 16, 256), jnp.bfloat16),
            pltpu.VMEM((used, GROUPS, 16, width), jnp.bfloat16),
            pltpu.VMEM((used, LAGS, width), jnp.float32),
            pltpu.VMEM((used, LAGS, width), jnp.bfloat16),
            dma((windows, 8)),
            dma((5,)),
            dma((windows, blocks)),
            dma((windows, blocks)),
            dma((3, windows, PIECES)),
            dma((3, windows, PIECES)),
            dma((4,)),
            dma((4,)),
            dma((3, 4)),
            dma((3, 4)),
            dma((used,)),
        ],
        compiler_params=pltpu.CompilerParams(collective_id=0, has_side_effects=True, vmem_limit_bytes=56 << 20),
    )(record, tables, basis, lags, offsets, sources)
    out = pl.pallas_call(
        duplicate,
        out_shape=jax.ShapeDtypeStruct(out.shape, out.dtype),
        in_specs=[anywhere],
        out_specs=anywhere,
        scratch_shapes=[pltpu.VMEM(out.shape, out.dtype), dma((used,)), dma((used,))],
    )(out)
    return out.reshape(ROUNDS, per, LAGS, width)


def solution(mesh):
    return jax.shard_map(
        body,
        mesh=mesh,
        in_specs=(P("win", "chan", None), P("win"), P()),
        out_specs=P(None, "win", None, "chan"),
        check_vma=False,
    )
```
